512 devices in a mesh: dom: 32 (over x, y), super: 16 (over z, core).
Axes of the slice: x: 4, y: 8, z: 8, core: 2. Of those that a mesh axis runs over, the one named last changes fastest.
Arguments:
- node_feats: bfloat16 [65536, 256], P(('dom', 'super')), may hold values from -6 to 6
- grad_out: bfloat16 [65536, 256], P(('dom', 'super')), may hold values from -6 to 6
- neighbours: int32 [65536, 32], P(('dom', 'super')), may hold values from 0 to 191
- cluster: int32 [65536], P(('dom', 'super')), may hold values from 0 to 63
- super_links: int32 [2048, 8], P('dom'), may hold values from 0 to 63, all different within a row
- w_query: bfloat16 [256, 256], replicated, may hold values from -0.375 to 0.375
- w_key: bfloat16 [256, 256], replicated, may hold values from -0.375 to 0.375
- w_value: bfloat16 [256, 256], replicated, may hold values from -0.375 to 0.375
- w_out: bfloat16 [256, 256], replicated, may hold values from -0.375 to 0.375
Outputs:
- grad_nodes: bfloat16 [65536, 256], P(('dom', 'super'))
- grad_weights: float32 [4, 256, 256], P(None, 'super')
The draws below stay inside these ranges and needn't reach their ends.
Inputs may be any that keep to these rules, and one draw needn't show every extreme that they name: `neighbours`: entries below 32 name the last 32 nodes of the previous block of the partition, the next 128 the block's own nodes, the rest the first 32 nodes of the following block, blocks taken cyclically. `cluster`: supernodes are numbered within the node's partition. `super_links`: each row names 8 different supernodes of the same partition.
All inputs are finite; a program needn't handle non-finite values.
Results may differ from the reference program's by a relative error of at most 0.013.
Values may be sent and summed in bfloat16 or wider, within the bound.
No kernel may reach another device: no remote copies, remote signals or barrier semaphores. Data moves between devices by JAX's collectives and lax.ppermute only.
A program may use at most 128 MiB of HBM per device.

```python
import math
import jax
import jax.numpy as jnp
import numpy as np
from jax import lax

WIDTH = 256
HEADS = 8
HEAD_DIM = 32
DEG = 32
K_TOP = 8
NODE_DEV = 128
HALO = 32
SUP_PART = 64
PART = 2048
NODES = 65536
SUPERS = 2048
N_DOM = 32


def touch_ends(array, rng, smallest, high):
    spot = [jax.random.randint(jax.random.fold_in(rng, axis), (), 0, length) for axis, length in enumerate(array.shape)]
    longest = array.shape.index(max(array.shape))
    neighbour = spot[:longest] + [(spot[longest] + 1) % array.shape[longest]] + spot[longest + 1:]
    return array.at[tuple(spot)].set(smallest).at[tuple(neighbour)].set(high)


def block_scale(own_key, shape, split, low, largest):
    level = 1.0
    for axis_at, parts in split:
        heights = jax.random.uniform(jax.random.fold_in(jax.random.fold_in(own_key, 6), axis_at), (parts,), jnp.float32, low / len(split), largest / len(split))
        level = level * jnp.repeat(jnp.exp(heights), shape[axis_at] // parts).reshape((-1,) + (1,) * (len(shape) - 1 - axis_at))
    return level


def rank_table(number_of, lean):
    loads = [(1 << 20) // math.isqrt(grade ** lean) + 1 for grade in range(1, number_of + 1)]
    scale = 1 + sum(loads) // (1 << 30)
    return np.cumsum(np.array([max(1, weight // scale) for weight in loads]))


def skewed_ids(own_key, extent, number_of, skew):
    listing = rank_table(number_of, skew)
    ticket = jax.random.randint(jax.random.fold_in(own_key, 1), extent, 0, int(listing[number_of - 1]))
    rank = jnp.searchsorted(jnp.asarray(listing, jnp.int32), ticket, side="right")
    return jax.random.permutation(jax.random.fold_in(own_key, 2), number_of)[rank].astype(jnp.int32)


def different_ones(rng, rows, number_of, top, lift):
    ranking = jax.random.permutation(jax.random.fold_in(rng, 1), number_of)
    boost = ranking
    for power in range(3):
        boost = boost * boost // number_of
    boost = boost * lift // number_of
    lots = jax.random.randint(jax.random.fold_in(rng, 2), (rows, number_of), 0, 4096) + boost
    holders = jax.random.permutation(jax.random.fold_in(rng, 3), rows)[jnp.arange(number_of) % rows]
    lots = jnp.where(jnp.arange(rows)[:, None] == holders[None, :], 1 << 14, lots)
    merit = lots * number_of + jnp.arange(number_of)
    return lax.top_k(merit.astype(jnp.int32), top)[1].astype(jnp.int32)


def noise(stream_key, shape, scale, limit, shards=(), kind=jnp.bfloat16):
    gain = block_scale(stream_key, shape, shards, -0.22, 0.18) if shards else 1.0
    values = jax.random.normal(stream_key, shape, jnp.float32) * scale * gain
    return jnp.minimum(jnp.maximum(values, -limit), limit).astype(kind)


def setup_inputs(seed: int = 0) -> dict:
    streams_of = jax.random.split(jax.random.key(seed), 10)
    node_feats = noise(streams_of[0], (NODES, WIDTH), 1.0, 6.0, ((0, 512),))
    grad_out = noise(streams_of[1], (NODES, WIDTH), 1.0, 6.0, ((0, 512),))
    neighbours = touch_ends(jax.random.randint(streams_of[2], (NODES, DEG), 0, NODE_DEV + 2 * HALO), jax.random.fold_in(streams_of[2], 1), 0, (NODE_DEV + 2 * HALO) - 1).astype(jnp.int32)
    cluster = touch_ends(skewed_ids(streams_of[3], (NODES,), SUP_PART, 2), jax.random.fold_in(streams_of[3], 3), 0, SUP_PART - 1).astype(jnp.int32)
    super_links = different_ones(streams_of[4], SUPERS, SUP_PART, K_TOP, 1024)
    w_query = noise(streams_of[5], (WIDTH, WIDTH), WIDTH ** -0.5, 0.375)
    w_key = noise(streams_of[6], (WIDTH, WIDTH), WIDTH ** -0.5, 0.375)
    w_value = noise(streams_of[7], (WIDTH, WIDTH), WIDTH ** -0.5, 0.375)
    w_out = noise(streams_of[8], (WIDTH, WIDTH), WIDTH ** -0.5, 0.375)
    return dict(node_feats=node_feats, grad_out=grad_out, neighbours=neighbours, cluster=cluster, super_links=super_links, w_query=w_query, w_key=w_key, w_value=w_value, w_out=w_out)


PRECISE = lax.Precision.HIGHEST

def softmax_last(scores):
    exponent = jnp.exp(scores)
    return exponent / lax.optimization_barrier(jnp.sum(exponent, -1, keepdims=True))

def to_half(argument):
    return lax.optimization_barrier(argument.astype(jnp.bfloat16)).astype(jnp.float32)

def neighbour_terms(queries, kv_table, row_index, grad_attn):
    rows_here = queries.shape[0]
    score_scale = 1.0 / math.sqrt(HEAD_DIM)
    gathered = jnp.take(kv_table, row_index.reshape(-1), axis=0).astype(jnp.float32)
    gathered = gathered.reshape(rows_here, DEG, 2, HEADS, HEAD_DIM)
    key_rows = gathered[:, :, 0]
    value_rows = gathered[:, :, 1]
    query_heads = queries.astype(jnp.float32).reshape(rows_here, HEADS, HEAD_DIM)
    grad_heads = grad_attn.astype(jnp.float32).reshape(rows_here, HEADS, HEAD_DIM)
    attn_prob = softmax_last(jnp.einsum('bhd,bjhd->bhj', query_heads, key_rows, precision=PRECISE) * score_scale)
    attn_weight = to_half(attn_prob)
    attended = jnp.einsum('bhj,bjhd->bhd', attn_weight, value_rows, precision=PRECISE).reshape(rows_here, WIDTH)
    grad_values = jnp.einsum('bhj,bhd->bjhd', attn_weight, grad_heads, precision=PRECISE)
    grad_prob = jnp.einsum('bhd,bjhd->bhj', grad_heads, value_rows, precision=PRECISE)
    grad_score = to_half(attn_prob * (grad_prob - lax.optimization_barrier(jnp.sum(attn_prob * grad_prob, -1, keepdims=True))) * score_scale)
    grad_query = jnp.einsum('bhj,bjhd->bhd', grad_score, key_rows, precision=PRECISE).reshape(rows_here, WIDTH)
    grad_keys = jnp.einsum('bhj,bhd->bjhd', grad_score, query_heads, precision=PRECISE)
    row_grads = jnp.stack([grad_keys, grad_values], 2).reshape(rows_here * DEG, 2 * WIDTH)
    return (attended, grad_query, row_grads)

def coarse_terms(queries, coarse_kv, grad_attn):
    rows_here = queries.shape[0]
    super_count = coarse_kv.shape[0]
    score_scale = 1.0 / math.sqrt(HEAD_DIM)
    key_heads = coarse_kv[:, :WIDTH].astype(jnp.float32).reshape(super_count, HEADS, HEAD_DIM)
    value_heads = coarse_kv[:, WIDTH:].astype(jnp.float32).reshape(super_count, HEADS, HEAD_DIM)
    query_heads = queries.astype(jnp.float32).reshape(rows_here, HEADS, HEAD_DIM)
    grad_heads = grad_attn.astype(jnp.float32).reshape(rows_here, HEADS, HEAD_DIM)
    attn_prob = softmax_last(jnp.einsum('bhd,shd->bhs', query_heads, key_heads, precision=PRECISE) * score_scale)
    attn_weight = to_half(attn_prob)
    attended = jnp.einsum('bhs,shd->bhd', attn_weight, value_heads, precision=PRECISE).reshape(rows_here, WIDTH)
    grad_values = jnp.einsum('bhs,bhd->shd', attn_weight, grad_heads, precision=PRECISE).reshape(super_count, WIDTH)
    grad_prob = jnp.einsum('bhd,shd->bhs', grad_heads, value_heads, precision=PRECISE)
    grad_score = to_half(attn_prob * (grad_prob - lax.optimization_barrier(jnp.sum(attn_prob * grad_prob, -1, keepdims=True))) * score_scale)
    grad_query = jnp.einsum('bhs,shd->bhd', grad_score, key_heads, precision=PRECISE).reshape(rows_here, WIDTH)
    grad_keys = jnp.einsum('bhs,bhd->shd', grad_score, query_heads, precision=PRECISE).reshape(super_count, WIDTH)
    return (attended, grad_query, jnp.concatenate([grad_keys, grad_values], 1))

def super_forward(pooled, pooled_proj, link_table):
    super_count = pooled.shape[0]
    score_scale = 1.0 / math.sqrt(HEAD_DIM)
    query_heads = pooled_proj[:, :WIDTH].astype(jnp.float32).reshape(super_count, HEADS, HEAD_DIM)
    linked = jnp.take(pooled_proj[:, WIDTH:], link_table.reshape(-1), axis=0).astype(jnp.float32)
    linked = linked.reshape(super_count, K_TOP, 2, HEADS, HEAD_DIM)
    key_rows = linked[:, :, 0]
    value_rows = linked[:, :, 1]
    attn_prob = softmax_last(jnp.einsum('shd,slhd->shl', query_heads, key_rows, precision=PRECISE) * score_scale)
    attn_weight = to_half(attn_prob)
    attended = jnp.einsum('shl,slhd->shd', attn_weight, value_rows, precision=PRECISE).reshape(super_count, WIDTH)
    super_state = (pooled.astype(jnp.float32) + attended).astype(jnp.bfloat16)
    return (super_state, (query_heads, key_rows, value_rows, attn_prob, attn_weight))

def super_backward(grad_state, link_table, saved_terms, stacked_t):
    query_heads, key_rows, value_rows, attn_prob, attn_weight = saved_terms
    super_count = grad_state.shape[0]
    score_scale = 1.0 / math.sqrt(HEAD_DIM)
    grad_heads = grad_state.reshape(super_count, HEADS, HEAD_DIM)
    grad_values = jnp.einsum('shl,shd->slhd', attn_weight, grad_heads, precision=PRECISE)
    grad_prob = jnp.einsum('shd,slhd->shl', grad_heads, value_rows, precision=PRECISE)
    grad_score = attn_prob * (grad_prob - lax.optimization_barrier(jnp.sum(attn_prob * grad_prob, -1, keepdims=True))) * score_scale
    grad_query = jnp.einsum('shl,slhd->shd', grad_score, key_rows, precision=PRECISE).reshape(super_count, WIDTH)
    grad_keys = jnp.einsum('shl,shd->slhd', grad_score, query_heads, precision=PRECISE)
    link_grads = jnp.stack([grad_keys, grad_values], 2).reshape(super_count * K_TOP, 2 * WIDTH)
    grad_kv = jax.ops.segment_sum(link_grads, link_table.reshape(-1), num_segments=super_count)
    grad_pooled_proj = jnp.concatenate([grad_query, grad_kv], 1)
    grad_pooled = grad_state + jnp.dot(grad_pooled_proj, stacked_t, precision=PRECISE)
    return (grad_pooled, grad_pooled_proj)

def partition_grads(node_feats, grad_out, neighbours, cluster, link_table, w_query, w_key, w_value, w_out):
    stacked = jnp.concatenate([w_query, w_key, w_value], 1)
    stacked_t = stacked.astype(jnp.float32).T
    projected = jnp.dot(node_feats, stacked, preferred_element_type=jnp.float32).astype(jnp.bfloat16)
    queries = projected[:, :WIDTH]
    kv_table = projected[:, WIDTH:]
    labels = jnp.arange(SUP_PART, dtype=jnp.int32)
    member = (cluster[None, :] == labels[:, None]).astype(jnp.float32)
    cluster_sums = jnp.dot(member, node_feats.astype(jnp.float32), precision=PRECISE)
    counts = lax.optimization_barrier(jnp.sum(member, 1))
    divisor = jnp.maximum(counts, 1.0)
    pooled = (cluster_sums / divisor[:, None]).astype(jnp.bfloat16)
    pooled_proj = jnp.dot(pooled, stacked, preferred_element_type=jnp.float32).astype(jnp.bfloat16)
    super_state, saved_terms = super_forward(pooled, pooled_proj, link_table)
    coarse = jnp.dot(super_state, stacked[:, WIDTH:], preferred_element_type=jnp.float32).astype(jnp.bfloat16)
    grad_attn = jnp.dot(grad_out, w_out.T, preferred_element_type=jnp.float32).astype(jnp.bfloat16)
    block_of = jnp.arange(PART, dtype=jnp.int32) // NODE_DEV
    neighbour_rows = ((block_of[:, None] * NODE_DEV + neighbours - HALO) % PART).astype(jnp.int32)
    block_rows = min(512, PART)

    def per_block(carry, offset):
        grad_table, coarse_grads = carry
        query_block = lax.dynamic_slice_in_dim(queries, offset, block_rows, 0)
        grad_block = lax.dynamic_slice_in_dim(grad_attn, offset, block_rows, 0)
        index_block = lax.dynamic_slice_in_dim(neighbour_rows, offset, block_rows, 0)
        near_out, near_query, near_rows = neighbour_terms(query_block, kv_table, index_block, grad_block)
        far_out, far_query, far_grads = coarse_terms(query_block, coarse, grad_block)
        grad_table = grad_table + jax.ops.segment_sum(near_rows, index_block.reshape(-1), num_segments=PART)
        return ((grad_table, coarse_grads + far_grads), (near_out + far_out, near_query + far_query))
    offsets = jnp.arange(PART // block_rows, dtype=jnp.int32) * block_rows
    start_carry = (jnp.zeros((PART, 2 * WIDTH), jnp.float32), jnp.zeros((SUP_PART, 2 * WIDTH), jnp.float32))
    (grad_table, coarse_grads), (attended, grad_query) = lax.scan(per_block, start_carry, offsets)
    attended = attended.reshape(PART, WIDTH).astype(jnp.bfloat16)
    grad_query = grad_query.reshape(PART, WIDTH)
    grad_wout = jnp.dot(attended.T, grad_out, preferred_element_type=jnp.float32)
    grad_state = jnp.dot(coarse_grads[:, :WIDTH], stacked_t[WIDTH:2 * WIDTH], precision=PRECISE)
    grad_state = grad_state + jnp.dot(coarse_grads[:, WIDTH:], stacked_t[2 * WIDTH:], precision=PRECISE)
    state_weights = jnp.dot(super_state.astype(jnp.float32).T, coarse_grads, precision=PRECISE)
    grad_pooled, grad_pooled_proj = super_backward(grad_state, link_table, saved_terms, stacked_t)
    super_weights = jnp.dot(pooled.astype(jnp.float32).T, grad_pooled_proj, precision=PRECISE)
    grad_proj = jnp.concatenate([grad_query, grad_table], 1).astype(jnp.bfloat16)
    spread = jnp.take(grad_pooled / divisor[:, None], cluster, axis=0)
    grad_nodes = grad_out.astype(jnp.float32) + jnp.dot(grad_proj, stacked.T, preferred_element_type=jnp.float32) + spread
    weights = jnp.dot(node_feats.T, grad_proj, preferred_element_type=jnp.float32) + super_weights
    weights = weights + jnp.concatenate([jnp.zeros((WIDTH, WIDTH), jnp.float32), state_weights], 1)
    stacked_grads = jnp.stack([weights[:, :WIDTH], weights[:, WIDTH:2 * WIDTH], weights[:, 2 * WIDTH:], grad_wout])
    return (grad_nodes.astype(jnp.bfloat16), stacked_grads)

def reference(node_feats, grad_out, neighbours, cluster, super_links, w_query, w_key, w_value, w_out):

    def one_partition(pieces):
        return partition_grads(pieces[0], pieces[1], pieces[2], pieces[3], pieces[4], w_query, w_key, w_value, w_out)
    pieces = (node_feats.reshape(N_DOM, PART, WIDTH), grad_out.reshape(N_DOM, PART, WIDTH), neighbours.reshape(N_DOM, PART, DEG), cluster.reshape(N_DOM, PART), super_links.reshape(N_DOM, SUP_PART, K_TOP))
    grad_nodes, weights = lax.map(one_partition, pieces)
    summed = lax.optimization_barrier(jnp.sum(weights, 0)) * (1.0 / math.sqrt(NODES))
    return (grad_nodes.reshape(NODES, WIDTH), summed)
```

```python
import functools
import math

import jax
import jax.numpy as jnp
from jax import lax
from jax.experimental import pallas as pl
from jax.experimental.pallas import tpu as pltpu
from jax.sharding import Mesh, PartitionSpec as P

WIDTH = 256
HEADS = 8
HEAD_DIM = 32
NODES = 128
HALO = 32
EXT = NODES + 2 * HALO
SUP = 64
SUM_ROWS = SUP + 16
STACK = HEADS * NODES
SCORE_SCALE = 1.0 / math.sqrt(HEAD_DIM)
NEVER = -1e30
BF = jnp.bfloat16
F32 = jnp.float32


def mm(a, b):
    return jnp.dot(a, b, preferred_element_type=F32)


def mm_nt(a, b):
    return lax.dot_general(a, b, (((1,), (1,)), ((), ())), preferred_element_type=F32)


def iota(shape, dim):
    return lax.broadcasted_iota(jnp.int32, shape, dim)


def flip(a):
    return a.astype(F32).T.astype(a.dtype)


def rows_of(h):
    return slice(h * HEAD_DIM, (h + 1) * HEAD_DIM)


def lanes_of(h):
    return slice(h * NODES, (h + 1) * NODES)


def stack_lanes(ref, flipped):
    ref[...] = jnp.zeros(ref.shape, ref.dtype)
    for h in range(HEADS):
        ref[rows_of(h), lanes_of(h)] = flipped[rows_of(h)]


def stack_rows(ref, rows):
    head = lax.shift_right_logical(iota(rows.shape, 1), 5)
    wide = rows.astype(F32)
    for h in range(HEADS):
        ref[lanes_of(h), :] = jnp.where(head == h, wide, 0.0).astype(rows.dtype)


def call(body, name, outs, scratch, flops, *args):
    size = sum(a.size * a.dtype.itemsize for a in args)
    return pl.pallas_call(
        body,
        name=name,
        out_shape=tuple(jax.ShapeDtypeStruct(s, d) for s, d in outs),
        scratch_shapes=[pltpu.VMEM(s, d) for s, d in scratch],
        compiler_params=pltpu.CompilerParams(vmem_limit_bytes=32 * 1024 * 1024),
        cost_estimate=pl.CostEstimate(flops=flops, bytes_accessed=size, transcendentals=0),
    )(*args)


def sums_body(x_ref, cluster_ref, out_ref):
    member = (cluster_ref[...] == iota((SUP, NODES), 0)).astype(F32)
    sums = mm(member.astype(BF), x_ref[...]).astype(BF)
    counts = jnp.sum(member, 1, keepdims=True)
    diagonal = iota((SUP, WIDTH), 0) == iota((SUP, WIDTH), 1)
    count_row = jnp.sum(jnp.where(diagonal, counts, 0.0), 0, keepdims=True)
    count_rows = jnp.broadcast_to(count_row, (SUM_ROWS - SUP, WIDTH)).astype(BF)
    for peer in range(out_ref.shape[0]):
        out_ref[peer, :SUP] = sums
        out_ref[peer, SUP:] = count_rows


def near_body(
    low_ref, x_ref, high_ref, grad_ref, slots_ref, wq_ref, wk_ref, wv_ref, wo_ref,
    q_ref, qt_ref, a_ref, at_ref, out_t_ref, gq_t_ref, wkv_ref, base_ref, back_low_ref, back_high_ref,
    q_lanes, a_lanes, q_rows, a_rows, weight_all, score_all,
):
    ext = jnp.concatenate([low_ref[...], x_ref[...], high_ref[...]], 0)
    wk = wk_ref[...]
    wv = wv_ref[...]
    queries = mm(x_ref[...], wq_ref[...]).astype(BF)
    keys = mm(ext, wk).astype(BF)
    vals = mm(ext, wv).astype(BF)
    grad_attn = mm_nt(grad_ref[...], wo_ref[...]).astype(BF)
    q_t = flip(queries)
    a_t = flip(grad_attn)
    keys_t = flip(keys)
    vals_t = flip(vals)
    q_ref[...] = queries
    qt_ref[...] = q_t
    a_ref[...] = grad_attn
    at_ref[...] = a_t
    stack_lanes(q_lanes, q_t)
    stack_lanes(a_lanes, a_t)
    stack_rows(q_rows, queries)
    stack_rows(a_rows, grad_attn)
    slots = slots_ref[...]
    row = iota((EXT, NODES), 0)
    count = jnp.zeros((EXT, NODES), F32)
    for j in range(slots.shape[0]):
        count = count + jnp.where(slots[j : j + 1] == row, 1.0, 0.0)
    log_count = jnp.where(count > 0.0, jnp.log(jnp.maximum(count, 1.0)), NEVER)
    for h in range(HEADS):
        score = mm(keys, q_lanes[:, lanes_of(h)])
        e = jnp.exp(score * SCORE_SCALE + log_count)
        prob = e * (1.0 / jnp.sum(e, 0, keepdims=True))
        weight = prob.astype(BF)
        g = mm(vals, a_lanes[:, lanes_of(h)])
        centre = jnp.sum(prob * g, 0, keepdims=True)
        d_score = (prob * (g - centre) * SCORE_SCALE).astype(BF)
        weight_all[:, lanes_of(h)] = weight
        score_all[:, lanes_of(h)] = d_score
        out_t_ref[rows_of(h)] = mm(vals_t[rows_of(h)], weight)
        gq_t_ref[rows_of(h)] = mm(keys_t[rows_of(h)], d_score)
    grad_keys = mm(score_all[...], q_rows[...]).astype(BF)
    grad_vals = mm(weight_all[...], a_rows[...]).astype(BF)
    ext_t = flip(ext)
    wkv_ref[0] = mm(ext_t, grad_keys)
    wkv_ref[1] = mm(ext_t, grad_vals)
    back = mm_nt(grad_keys, wk) + mm_nt(grad_vals, wv)
    base_ref[...] = grad_ref[...].astype(F32) + back[HALO : HALO + NODES]
    back_low_ref[...] = back[:HALO].astype(BF)
    back_high_ref[...] = back[HALO + NODES :].astype(BF)


def far_body(
    parts_ref, links_ref, x_ref, grad_ref, wq_ref, wk_ref, wv_ref,
    q_ref, qt_ref, a_ref, at_ref, near_t_ref, near_gq_ref, wkv_ref, base_ref,
    weights_ref, pooled_grad_ref, nodes_ref,
    lanes_a, lanes_b, rows_a, rows_b, weight_all, score_all, s_weight, s_prob, s_score, s_rows,
):
    wq = wq_ref[...]
    wk = wk_ref[...]
    wv = wv_ref[...]
    totals = jnp.sum(parts_ref[...].astype(F32), 0)
    diagonal = iota((SUP, WIDTH), 0) == iota((SUP, WIDTH), 1)
    counts = jnp.sum(jnp.where(diagonal, totals[SUP : SUP + 1], 0.0), 1, keepdims=True)
    inverse = 1.0 / jnp.maximum(counts, 1.0)
    pooled = (totals[:SUP] * inverse).astype(BF)
    pad = jnp.zeros((NODES - SUP, WIDTH), BF)

    s_q = jnp.concatenate([mm(pooled, wq).astype(BF), pad], 0)
    s_k = mm(pooled, wk).astype(BF)
    s_v = mm(pooled, wv).astype(BF)
    s_kt = flip(s_k)
    s_vt = flip(s_v)
    stack_lanes(lanes_a, flip(s_q))
    stack_rows(s_rows, s_q)
    links = links_ref[...]
    target = iota((SUP, NODES), 0)
    linked = iota((SUP, NODES), 1) >= SUP
    for l in range(links.shape[0]):
        linked = jnp.logical_or(linked, links[l : l + 1] == target)
    allowed = jnp.where(linked, 0.0, NEVER)
    state_t = []
    for h in range(HEADS):
        e = jnp.exp(mm(s_k, lanes_a[:, lanes_of(h)]) * SCORE_SCALE + allowed)
        prob = e * (1.0 / jnp.sum(e, 0, keepdims=True))
        weight = prob.astype(BF)
        s_prob[:, lanes_of(h)] = prob
        s_weight[:, lanes_of(h)] = weight
        state_t.append(mm(s_vt[rows_of(h)], weight))
    state = (pooled.astype(F32) + jnp.concatenate(state_t, 0).T[:SUP]).astype(BF)

    c_k = mm(state, wk).astype(BF)
    c_v = mm(state, wv).astype(BF)
    c_kt = flip(c_k)
    c_vt = flip(c_v)
    stack_lanes(lanes_a, qt_ref[...])
    stack_lanes(lanes_b, at_ref[...])
    stack_rows(rows_a, q_ref[...])
    stack_rows(rows_b, a_ref[...])
    out_t = []
    gq_t = []
    for h in range(HEADS):
        e = jnp.exp(mm(c_k, lanes_a[:, lanes_of(h)]) * SCORE_SCALE)
        prob = e * (1.0 / jnp.sum(e, 0, keepdims=True))
        weight = prob.astype(BF)
        g = mm(c_v, lanes_b[:, lanes_of(h)])
        centre = jnp.sum(prob * g, 0, keepdims=True)
        d_score = (prob * (g - centre) * SCORE_SCALE).astype(BF)
        weight_all[:, lanes_of(h)] = weight
        score_all[:, lanes_of(h)] = d_score
        out_t.append(mm(c_vt[rows_of(h)], weight))
        gq_t.append(mm(c_kt[rows_of(h)], d_score))
    grad_ck = mm(score_all[...], rows_a[...]).astype(BF)
    grad_cv = mm(weight_all[...], rows_b[...]).astype(BF)

    grad_state = mm_nt(grad_ck, wk) + mm_nt(grad_cv, wv)
    gs = jnp.concatenate([grad_state.astype(BF), pad], 0)
    stack_lanes(lanes_b, flip(gs))
    stack_rows(rows_b, gs)
    gsq_t = []
    for h in range(HEADS):
        prob = s_prob[:, lanes_of(h)]
        g = mm(s_v, lanes_b[:, lanes_of(h)])
        centre = jnp.sum(prob * g, 0, keepdims=True)
        d_score = (prob * (g - centre) * SCORE_SCALE).astype(BF)
        s_score[:, lanes_of(h)] = d_score
        gsq_t.append(mm(s_kt[rows_of(h)], d_score))
    gsq = jnp.concatenate(gsq_t, 0).T[:SUP].astype(BF)
    gsk = mm(s_score[...], s_rows[...]).astype(BF)
    gsv = mm(s_weight[...], rows_b[...]).astype(BF)
    projections = jnp.concatenate([wq, wk, wv], 1)
    grad_pooled = grad_state + mm_nt(jnp.concatenate([gsq, gsk, gsv], 1), projections)
    pooled_grad_ref[...] = (grad_pooled * inverse).astype(BF)

    gq = (near_gq_ref[...] + jnp.concatenate(gq_t, 0)).T.astype(BF)
    attended_t = (near_t_ref[...] + jnp.concatenate(out_t, 0)).astype(BF)
    pooled_t = flip(pooled)
    state_flip = flip(state)
    weights_ref[0] = (mm(flip(x_ref[...]), gq) + mm(pooled_t, gsq)).astype(BF)
    weights_ref[1] = (wkv_ref[0] + mm(pooled_t, gsk) + mm(state_flip, grad_ck)).astype(BF)
    weights_ref[2] = (wkv_ref[1] + mm(pooled_t, gsv) + mm(state_flip, grad_cv)).astype(BF)
    weights_ref[3] = mm(attended_t, grad_ref[...]).astype(BF)
    nodes_ref[...] = base_ref[...] + mm_nt(gq, wq)


def final_body(scale, parts_ref, out_ref):
    rows = parts_ref.shape[0] // out_ref.shape[0]
    for w in range(out_ref.shape[0]):
        part = parts_ref[w * rows : (w + 1) * rows].astype(F32)
        out_ref[w] = jnp.sum(part, 0) * scale


def nodes_body(pieces_ref, base_ref, low_ref, high_ref, parts_ref, cluster_ref, share_ref, out_ref):
    share = jnp.sum(pieces_ref[...].astype(F32), 0).astype(BF)
    for peer in range(share_ref.shape[0]):
        share_ref[peer] = share
    grad_pooled = jnp.sum(parts_ref[...].astype(F32), 0)
    coarse = grad_pooled.astype(BF)
    fine = (grad_pooled - coarse.astype(F32)).astype(BF)
    member = (cluster_ref[...] == iota((SUP, NODES), 0)).astype(F32).T.astype(BF)
    spread = mm(jnp.concatenate([member, member], 1), jnp.concatenate([coarse, fine], 0))
    total = base_ref[...] + spread
    out_ref[:HALO] = (total[:HALO] + low_ref[...].astype(F32)).astype(BF)
    out_ref[HALO : NODES - HALO] = total[HALO : NODES - HALO].astype(BF)
    out_ref[NODES - HALO :] = (total[NODES - HALO :] + high_ref[...].astype(F32)).astype(BF)


def swap(parts, axes):
    return lax.all_to_all(parts, axes, 0, 0, tiled=True)


def local(sizes, node_feats, grad_out, neighbours, cluster, super_links, w_query, w_key, w_value, w_out):
    n_x, n_y, n_z, n_c = sizes
    n_super = n_z * n_c
    n_dom = n_x * n_y
    supers = ("z", "c")
    up = [(i, (i + 1) % n_super) for i in range(n_super)]
    down = [(i, (i + n_super - 1) % n_super) for i in range(n_super)]
    cluster_row = cluster.reshape(1, NODES)
    (sums,) = call(
        sums_body, "cluster_sums", [((n_super, SUM_ROWS, WIDTH), BF)], [], 1 << 22, node_feats, cluster_row
    )
    low = lax.ppermute(node_feats[NODES - HALO :], supers, up)
    high = lax.ppermute(node_feats[:HALO], supers, down)
    sums, low, high = lax.optimization_barrier((sums, low, high))
    parts = swap(sums, supers)
    q, q_t, a, a_t, near_t, near_gq, wkv, base, back_low, back_high = call(
        near_body,
        "near_attention",
        [
            ((NODES, WIDTH), BF), ((WIDTH, NODES), BF), ((NODES, WIDTH), BF), ((WIDTH, NODES), BF),
            ((WIDTH, NODES), F32), ((WIDTH, NODES), F32), ((2, WIDTH, WIDTH), F32), ((NODES, WIDTH), F32),
            ((HALO, WIDTH), BF), ((HALO, WIDTH), BF),
        ],
        [
            ((WIDTH, STACK), BF), ((WIDTH, STACK), BF), ((STACK, WIDTH), BF), ((STACK, WIDTH), BF),
            ((EXT, STACK), BF), ((EXT, STACK), BF),
        ],
        10 << 30,
        low, node_feats, high, grad_out, neighbours.T, w_query, w_key, w_value, w_out,
    )
    from_high = lax.ppermute(back_low, supers, down)
    from_low = lax.ppermute(back_high, supers, up)
    links = jnp.pad(super_links.T, ((0, 0), (0, NODES - SUP)))
    weights, pooled_share, own = call(
        far_body,
        "far_attention",
        [((4, WIDTH, WIDTH), BF), ((SUP, WIDTH), BF), ((NODES, WIDTH), F32)],
        [
            ((WIDTH, STACK), BF), ((WIDTH, STACK), BF), ((STACK, WIDTH), BF), ((STACK, WIDTH), BF),
            ((SUP, STACK), BF), ((SUP, STACK), BF), ((SUP, STACK), BF), ((SUP, STACK), F32), ((SUP, STACK), BF),
            ((STACK, WIDTH), BF),
        ],
        10 << 30,
        parts, links, node_feats, grad_out, w_query, w_key, w_value,
        q, q_t, a, a_t, near_t, near_gq, wkv, base,
    )
    share_rows = WIDTH // n_super
    pieces = swap(weights.reshape(4 * n_super, share_rows, WIDTH), ("x",) + supers)
    pooled_parts = lax.all_gather(pooled_share, supers)
    shares, grad_nodes = call(
        nodes_body,
        "grad_nodes",
        [((n_dom, share_rows, WIDTH), BF), ((NODES, WIDTH), BF)],
        [],
        1 << 30,
        pieces, own, from_low, from_high, pooled_parts, cluster_row,
    )
    shares = swap(shares, ("x", "y"))
    scale = 1.0 / math.sqrt(NODES * n_super * n_dom)
    (grad_weights,) = call(
        functools.partial(final_body, scale), "grad_weights", [((4, share_rows, WIDTH), F32)], [], 1 << 20, shares
    )
    return grad_nodes, grad_weights


def solution(mesh):
    n_dom = mesh.shape["dom"]
    n_super = mesh.shape["super"]
    sizes = (4, n_dom // 4, n_super // 2, 2)
    fine = Mesh(mesh.devices.reshape(sizes), ("x", "y", "z", "c"))
    everyone = ("x", "y", "z", "c")
    return jax.shard_map(
        functools.partial(local, sizes),
        mesh=fine,
        in_specs=(
            P(everyone, None),
            P(everyone, None),
            P(everyone, None),
            P(everyone),
            P(("x", "y"), None),
            P(),
            P(),
            P(),
            P(),
        ),
        out_specs=(P(everyone, None), P(None, ("z", "c"), None)),
        check_vma=False,
    )
```

```python
import functools
import math

import jax
import jax.numpy as jnp
from jax import lax
from jax.experimental import pallas as pl
from jax.experimental.pallas import tpu as pltpu
from jax.sharding import Mesh, PartitionSpec as P

WIDTH = 256
HEADS = 8
HEAD_DIM = 32
NODES = 128
HALO = 32
EXT = NODES + 2 * HALO
SUP = 64
SUM_ROWS = SUP + 16
STACK = HEADS * NODES
SCORE_SCALE = 1.0 / math.sqrt(HEAD_DIM)
NEVER = -1e30
BF = jnp.bfloat16
F32 = jnp.float32


def mm(a, b):
    return jnp.dot(a, b, preferred_element_type=F32)


def mm_nt(a, b):
    return lax.dot_general(a, b, (((1,), (1,)), ((), ())), preferred_element_type=F32)


def iota(shape, dim):
    return lax.broadcasted_iota(jnp.int32, shape, dim)


def flip(a):
    return a.astype(F32).T.astype(a.dtype)


def rows_of(h):
    return slice(h * HEAD_DIM, (h + 1) * HEAD_DIM)


def lanes_of(h):
    return slice(h * NODES, (h + 1) * NODES)


def stack_lanes(ref, flipped):
    ref[...] = jnp.zeros(ref.shape, ref.dtype)
    for h in range(HEADS):
        ref[rows_of(h), lanes_of(h)] = flipped[rows_of(h)]


def stack_rows(ref, rows):
    head = lax.shift_right_logical(iota(rows.shape, 1), 5)
    wide = rows.astype(F32)
    for h in range(HEADS):
        ref[lanes_of(h), :] = jnp.where(head == h, wide, 0.0).astype(rows.dtype)


def call(body, name, outs, scratch, flops, *args):
    size = sum(a.size * a.dtype.itemsize for a in args)
    vmem = pl.BlockSpec(memory_space=pltpu.VMEM)
    smem = pl.BlockSpec(memory_space=pltpu.SMEM)
    return pl.pallas_call(
        body,
        in_specs=[smem if a.ndim == 1 else vmem for a in args],
        name=name,
        out_shape=tuple(jax.ShapeDtypeStruct(s, d) for s, d in outs),
        scratch_shapes=[pltpu.VMEM(s, d) for s, d in scratch],
        compiler_params=pltpu.CompilerParams(vmem_limit_bytes=32 * 1024 * 1024),
        cost_estimate=pl.CostEstimate(flops=flops, bytes_accessed=size, transcendentals=0),
    )(*args)


def sums_body(x_ref, cluster_ref, out_ref):
    member = (cluster_ref[...] == iota((SUP, NODES), 0)).astype(F32)
    sums = mm(member.astype(BF), x_ref[...])
    counts = jnp.sum(member, 1, keepdims=True)
    diagonal = iota((SUP, WIDTH), 0) == iota((SUP, WIDTH), 1)
    count_row = jnp.sum(jnp.where(diagonal, counts, 0.0), 0, keepdims=True)
    out_ref[:SUP] = sums
    out_ref[SUP:] = jnp.broadcast_to(count_row, (SUM_ROWS - SUP, WIDTH))


def chip_sums_body(parts_ref, out_ref):
    total = (parts_ref[0] + parts_ref[1]).astype(BF)
    for peer in range(out_ref.shape[0]):
        out_ref[peer] = total


def near_body(
    low_ref, x_ref, high_ref, grad_ref, slots_ref, wq_ref, wk_ref, wv_ref, wo_ref,
    q_ref, qt_ref, a_ref, at_ref, out_t_ref, gq_t_ref, wkv_ref, base_ref, back_low_ref, back_high_ref,
    q_lanes, a_lanes, q_rows, a_rows, weight_all, score_all,
):
    ext = jnp.concatenate([low_ref[...], x_ref[...], high_ref[...]], 0)
    wk = wk_ref[...]
    wv = wv_ref[...]
    queries = mm(x_ref[...], wq_ref[...]).astype(BF)
    keys = mm(ext, wk).astype(BF)
    vals = mm(ext, wv).astype(BF)
    grad_attn = mm_nt(grad_ref[...], wo_ref[...]).astype(BF)
    q_t = flip(queries)
    a_t = flip(grad_attn)
    keys_t = flip(keys)
    vals_t = flip(vals)
    q_ref[...] = queries
    qt_ref[...] = q_t
    a_ref[...] = grad_attn
    at_ref[...] = a_t
    stack_lanes(q_lanes, q_t)
    stack_lanes(a_lanes, a_t)
    stack_rows(q_rows, queries)
    stack_rows(a_rows, grad_attn)
    slots = slots_ref[...]
    row = iota((EXT, NODES), 0)
    count = jnp.zeros((EXT, NODES), F32)
    for j in range(slots.shape[0]):
        count = count + jnp.where(slots[j : j + 1] == row, 1.0, 0.0)
    log_count = jnp.where(count > 0.0, jnp.log(jnp.maximum(count, 1.0)), NEVER)
    for h in range(HEADS):
        score = mm(keys, q_lanes[:, lanes_of(h)])
        e = jnp.exp(score * SCORE_SCALE + log_count)
        prob = e * (1.0 / jnp.sum(e, 0, keepdims=True))
        weight = prob.astype(BF)
        g = mm(vals, a_lanes[:, lanes_of(h)])
        centre = jnp.sum(prob * g, 0, keepdims=True)
        d_score = (prob * (g - centre) * SCORE_SCALE).astype(BF)
        weight_all[:, lanes_of(h)] = weight
        score_all[:, lanes_of(h)] = d_score
        out_t_ref[rows_of(h)] = mm(vals_t[rows_of(h)], weight)
        gq_t_ref[rows_of(h)] = mm(keys_t[rows_of(h)], d_score)
    grad_keys = mm(score_all[...], q_rows[...]).astype(BF)
    grad_vals = mm(weight_all[...], a_rows[...]).astype(BF)
    ext_t = flip(ext)
    wkv_ref[0] = mm(ext_t, grad_keys)
    wkv_ref[1] = mm(ext_t, grad_vals)
    back = mm_nt(grad_keys, wk) + mm_nt(grad_vals, wv)
    base_ref[...] = grad_ref[...].astype(F32) + back[HALO : HALO + NODES]
    back_low_ref[...] = back[:HALO].astype(BF)
    back_high_ref[...] = back[HALO + NODES :].astype(BF)


def far_body(
    parts_ref, links_ref, x_ref, grad_ref, wq_ref, wk_ref, wv_ref,
    q_ref, qt_ref, a_ref, at_ref, near_t_ref, near_gq_ref, wkv_ref, base_ref, core_ref,
    mine_ref, mine_pooled_ref, theirs_ref, nodes_ref,
    lanes_a, lanes_b, rows_a, rows_b, weight_all, score_all, s_weight, s_prob, s_score, s_rows,
):
    wq = wq_ref[...]
    wk = wk_ref[...]
    wv = wv_ref[...]
    totals = jnp.sum(parts_ref[...].astype(F32), 0)
    diagonal = iota((SUP, WIDTH), 0) == iota((SUP, WIDTH), 1)
    counts = jnp.sum(jnp.where(diagonal, totals[SUP : SUP + 1], 0.0), 1, keepdims=True)
    inverse = 1.0 / jnp.maximum(counts, 1.0)
    pooled = (totals[:SUP] * inverse).astype(BF)
    pad = jnp.zeros((NODES - SUP, WIDTH), BF)

    s_q = jnp.concatenate([mm(pooled, wq).astype(BF), pad], 0)
    s_k = mm(pooled, wk).astype(BF)
    s_v = mm(pooled, wv).astype(BF)
    s_kt = flip(s_k)
    s_vt = flip(s_v)
    stack_lanes(lanes_a, flip(s_q))
    stack_rows(s_rows, s_q)
    links = links_ref[...]
    target = iota((SUP, NODES), 0)
    linked = iota((SUP, NODES), 1) >= SUP
    for l in range(links.shape[0]):
        linked = jnp.logical_or(linked, links[l : l + 1] == target)
    allowed = jnp.where(linked, 0.0, NEVER)
    state_t = []
    for h in range(HEADS):
        e = jnp.exp(mm(s_k, lanes_a[:, lanes_of(h)]) * SCORE_SCALE + allowed)
        prob = e * (1.0 / jnp.sum(e, 0, keepdims=True))
        weight = prob.astype(BF)
        s_prob[:, lanes_of(h)] = prob
        s_weight[:, lanes_of(h)] = weight
        state_t.append(mm(s_vt[rows_of(h)], weight))
    state = (pooled.astype(F32) + jnp.concatenate(state_t, 0).T[:SUP]).astype(BF)

    c_k = mm(state, wk).astype(BF)
    c_v = mm(state, wv).astype(BF)
    c_kt = flip(c_k)
    c_vt = flip(c_v)
    stack_lanes(lanes_a, qt_ref[...])
    stack_lanes(lanes_b, at_ref[...])
    stack_rows(rows_a, q_ref[...])
    stack_rows(rows_b, a_ref[...])
    out_t = []
    gq_t = []
    for h in range(HEADS):
        e = jnp.exp(mm(c_k, lanes_a[:, lanes_of(h)]) * SCORE_SCALE)
        prob = e * (1.0 / jnp.sum(e, 0, keepdims=True))
        weight = prob.astype(BF)
        g = mm(c_v, lanes_b[:, lanes_of(h)])
        centre = jnp.sum(prob * g, 0, keepdims=True)
        d_score = (prob * (g - centre) * SCORE_SCALE).astype(BF)
        weight_all[:, lanes_of(h)] = weight
        score_all[:, lanes_of(h)] = d_score
        out_t.append(mm(c_vt[rows_of(h)], weight))
        gq_t.append(mm(c_kt[rows_of(h)], d_score))
    grad_ck = mm(score_all[...], rows_a[...]).astype(BF)
    grad_cv = mm(weight_all[...], rows_b[...]).astype(BF)

    grad_state = mm_nt(grad_ck, wk) + mm_nt(grad_cv, wv)
    gs = jnp.concatenate([grad_state.astype(BF), pad], 0)
    stack_lanes(lanes_b, flip(gs))
    stack_rows(rows_b, gs)
    gsq_t = []
    for h in range(HEADS):
        prob = s_prob[:, lanes_of(h)]
        g = mm(s_v, lanes_b[:, lanes_of(h)])
        centre = jnp.sum(prob * g, 0, keepdims=True)
        d_score = (prob * (g - centre) * SCORE_SCALE).astype(BF)
        s_score[:, lanes_of(h)] = d_score
        gsq_t.append(mm(s_kt[rows_of(h)], d_score))
    gsq = jnp.concatenate(gsq_t, 0).T[:SUP].astype(BF)
    gsk = mm(s_score[...], s_rows[...]).astype(BF)
    gsv = mm(s_weight[...], rows_b[...]).astype(BF)
    projections = jnp.concatenate([wq, wk, wv], 1)
    grad_pooled = grad_state + mm_nt(jnp.concatenate([gsq, gsk, gsv], 1), projections)
    share = grad_pooled * inverse

    gq = (near_gq_ref[...] + jnp.concatenate(gq_t, 0)).T.astype(BF)
    attended_t = (near_t_ref[...] + jnp.concatenate(out_t, 0)).astype(BF)
    pooled_t = flip(pooled)
    state_flip = flip(state)
    grads = [
        mm(flip(x_ref[...]), gq) + mm(pooled_t, gsq),
        wkv_ref[0] + mm(pooled_t, gsk) + mm(state_flip, grad_ck),
        wkv_ref[1] + mm(pooled_t, gsv) + mm(state_flip, grad_cv),
        mm(attended_t, grad_ref[...]),
    ]
    core = core_ref[0]
    groups = mine_ref.shape[1]
    rows = mine_ref.shape[2]
    first = jnp.broadcast_to(core, (groups, rows, WIDTH)) == 0
    for w in range(4):
        pairs = grads[w].reshape(groups, 2, rows, WIDTH)
        low, high = pairs[:, 0], pairs[:, 1]
        mine_ref[w] = jnp.where(first, low, high)
        theirs_ref[w * groups * rows : (w + 1) * groups * rows] = (
            jnp.where(first, high, low).reshape(groups * rows, WIDTH).astype(BF)
        )
    half = SUP // 2
    first = jnp.broadcast_to(core, (half, WIDTH)) == 0
    mine_pooled_ref[...] = jnp.where(first, share[:half], share[half:])
    theirs_ref[4 * groups * rows :] = jnp.where(first, share[half:], share[:half]).astype(BF)
    nodes_ref[...] = base_ref[...] + mm_nt(gq, wq)


def final_body(scale, parts_ref, out_ref):
    rows = parts_ref.shape[0] // out_ref.shape[0]
    for w in range(out_ref.shape[0]):
        part = parts_ref[w * rows : (w + 1) * rows].astype(F32)
        out_ref[w] = jnp.sum(part, 0) * scale


def chip_grads_body(mine_ref, mine_pooled_ref, both_ref, core_ref, weights_ref, pooled_ref):
    received = both_ref[1 - core_ref[0]].astype(F32)
    size = received.shape[0] - mine_pooled_ref.shape[0]
    weights_ref[...] = (mine_ref[...] + received[:size].reshape(mine_ref.shape)).astype(BF)
    pooled_ref[...] = (mine_pooled_ref[...] + received[size:]).astype(BF)


def nodes_body(pieces_ref, base_ref, low_ref, high_ref, parts_ref, cluster_ref, share_ref, out_ref):
    share = jnp.sum(pieces_ref[...].astype(F32), 0).astype(BF)
    for peer in range(share_ref.shape[0]):
        share_ref[peer] = share
    parts = parts_ref[...].astype(F32)
    parts = parts.reshape(parts.shape[0] // 2, 2 * parts.shape[1], WIDTH)
    grad_pooled = jnp.sum(parts, 0)
    coarse = grad_pooled.astype(BF)
    fine = (grad_pooled - coarse.astype(F32)).astype(BF)
    member = (cluster_ref[...] == iota((SUP, NODES), 0)).astype(F32).T.astype(BF)
    spread = mm(jnp.concatenate([member, member], 1), jnp.concatenate([coarse, fine], 0))
    total = base_ref[...] + spread
    out_ref[:HALO] = (total[:HALO] + low_ref[...].astype(F32)).astype(BF)
    out_ref[HALO : NODES - HALO] = total[HALO : NODES - HALO].astype(BF)
    out_ref[NODES - HALO :] = (total[NODES - HALO :] + high_ref[...].astype(F32)).astype(BF)


def swap(parts, axes):
    return lax.all_to_all(parts, axes, 0, 0, tiled=True)


def local(sizes, node_feats, grad_out, neighbours, cluster, super_links, w_query, w_key, w_value, w_out):
    n_x, n_y, n_z, n_c = sizes
    n_super = n_z * n_c
    n_dom = n_x * n_y
    supers = ("z", "c")
    up = [(i, (i + 1) % n_super) for i in range(n_super)]
    down = [(i, (i + n_super - 1) % n_super) for i in range(n_super)]
    cluster_row = cluster.reshape(1, NODES)
    (sums,) = call(
        sums_body, "cluster_sums", [((SUM_ROWS, WIDTH), F32)], [], 1 << 22, node_feats, cluster_row
    )
    (sums,) = call(
        chip_sums_body, "chip_sums", [((n_z, SUM_ROWS, WIDTH), BF)], [], 1 << 20, lax.all_gather(sums, "c")
    )
    core = lax.axis_index("c").reshape(1)
    low = lax.ppermute(node_feats[NODES - HALO :], supers, up)
    high = lax.ppermute(node_feats[:HALO], supers, down)
    parts = swap(sums, "z")
    q, q_t, a, a_t, near_t, near_gq, wkv, base, back_low, back_high = call(
        near_body,
        "near_attention",
        [
            ((NODES, WIDTH), BF), ((WIDTH, NODES), BF), ((NODES, WIDTH), BF), ((WIDTH, NODES), BF),
            ((WIDTH, NODES), F32), ((WIDTH, NODES), F32), ((2, WIDTH, WIDTH), F32), ((NODES, WIDTH), F32),
            ((HALO, WIDTH), BF), ((HALO, WIDTH), BF),
        ],
        [
            ((WIDTH, STACK), BF), ((WIDTH, STACK), BF), ((STACK, WIDTH), BF), ((STACK, WIDTH), BF),
            ((EXT, STACK), BF), ((EXT, STACK), BF),
        ],
        10 << 30,
        low, node_feats, high, grad_out, neighbours.T, w_query, w_key, w_value, w_out,
    )
    from_high = lax.ppermute(back_low, supers, down)
    from_low = lax.ppermute(back_high, supers, up)
    links = jnp.pad(super_links.T, ((0, 0), (0, NODES - SUP)))
    share_rows = WIDTH // n_super
    weight_rows = 4 * n_z * share_rows
    mine, mine_pooled, theirs, own = call(
        far_body,
        "far_attention",
        [
            ((4, n_z, share_rows, WIDTH), F32), ((SUP // 2, WIDTH), F32),
            ((weight_rows + SUP // 2, WIDTH), BF), ((NODES, WIDTH), F32),
        ],
        [
            ((WIDTH, STACK), BF), ((WIDTH, STACK), BF), ((STACK, WIDTH), BF), ((STACK, WIDTH), BF),
            ((SUP, STACK), BF), ((SUP, STACK), BF), ((SUP, STACK), BF), ((SUP, STACK), F32), ((SUP, STACK), BF),
            ((STACK, WIDTH), BF),
        ],
        10 << 30,
        parts, links, node_feats, grad_out, w_query, w_key, w_value,
        q, q_t, a, a_t, near_t, near_gq, wkv, base, core,
    )
    weights, pooled_share = call(
        chip_grads_body,
        "chip_grads",
        [((4, n_z, share_rows, WIDTH), BF), ((SUP // 2, WIDTH), BF)],
        [],
        1 << 20,
        mine, mine_pooled, lax.all_gather(theirs, "c"), core,
    )
    pieces = swap(weights.reshape(4 * n_z, share_rows, WIDTH), ("x", "z"))
    pooled_parts = lax.all_gather(pooled_share, supers)
    shares, grad_nodes = call(
        nodes_body,
        "grad_nodes",
        [((n_dom, share_rows, WIDTH), BF), ((NODES, WIDTH), BF)],
        [],
        1 << 30,
        pieces, own, from_low, from_high, pooled_parts, cluster_row,
    )
    shares = swap(shares, ("x", "y"))
    scale = 1.0 / math.sqrt(NODES * n_super * n_dom)
    (grad_weights,) = call(
        functools.partial(final_body, scale), "grad_weights", [((4, share_rows, WIDTH), F32)], [], 1 << 20, shares
    )
    return grad_nodes, grad_weights


def solution(mesh):
    n_dom = mesh.shape["dom"]
    n_super = mesh.shape["super"]
    sizes = (4, n_dom // 4, n_super // 2, 2)
    fine = Mesh(mesh.devices.reshape(sizes), ("x", "y", "z", "c"))
    everyone = ("x", "y", "z", "c")
    return jax.shard_map(
        functools.partial(local, sizes),
        mesh=fine,
        in_specs=(
            P(everyone, None),
            P(everyone, None),
            P(everyone, None),
            P(everyone),
            P(("x", "y"), None),
            P(),
            P(),
            P(),
            P(),
        ),
        out_specs=(P(everyone, None), P(None, ("z", "c"), None)),
        check_vma=False,
    )
```

```python
import functools
import math

import jax
import jax.numpy as jnp
from jax import lax
from jax.experimental import pallas as pl
from jax.experimental.pallas import tpu as pltpu
from jax.sharding import Mesh, PartitionSpec as P

WIDTH = 256
HEADS = 8
HEAD_DIM = 32
NODES = 128
HALO = 32
EXT = NODES + 2 * HALO
SUP = 64
SUM_ROWS = SUP + 8
STACK = HEADS * NODES
SCORE_SCALE = 1.0 / math.sqrt(HEAD_DIM)
NEVER = -1e30
BF = jnp.bfloat16
F32 = jnp.float32


def mm(a, b):
    return jnp.dot(a, b, preferred_element_type=F32)


def mm_nt(a, b):
    return lax.dot_general(a, b, (((1,), (1,)), ((), ())), preferred_element_type=F32)


def iota(shape, dim):
    return lax.broadcasted_iota(jnp.int32, shape, dim)


def flip(a):
    return a.astype(F32).T.astype(a.dtype)


def rows_of(h):
    return slice(h * HEAD_DIM, (h + 1) * HEAD_DIM)


def lanes_of(h):
    return slice(h * NODES, (h + 1) * NODES)


def stack_lanes(ref, flipped):
    ref[...] = jnp.zeros(ref.shape, ref.dtype)
    for h in range(HEADS):
        ref[rows_of(h), lanes_of(h)] = flipped[rows_of(h)]


def stack_rows(ref, rows):
    head = lax.shift_right_logical(iota(rows.shape, 1), 5)
    wide = rows.astype(F32)
    for h in range(HEADS):
        ref[lanes_of(h), :] = jnp.where(head == h, wide, 0.0).astype(rows.dtype)


def call(body, name, outs, scratch, flops, *args, outside=()):
    size = sum(a.size * a.dtype.itemsize for a in args)
    vmem = pl.BlockSpec(memory_space=pltpu.VMEM)
    smem = pl.BlockSpec(memory_space=pltpu.SMEM)
    anywhere = pl.BlockSpec(memory_space=pltpu.HBM)
    return pl.pallas_call(
        body,
        in_specs=[anywhere if i in outside else smem if a.ndim == 1 else vmem for i, a in enumerate(args)],
        name=name,
        out_shape=tuple(jax.ShapeDtypeStruct(s, d) for s, d in outs),
        scratch_shapes=[pltpu.VMEM(*s) if isinstance(s, tuple) else s for s in scratch],
        compiler_params=pltpu.CompilerParams(vmem_limit_bytes=32 * 1024 * 1024),
        cost_estimate=pl.CostEstimate(flops=flops, bytes_accessed=size, transcendentals=0),
    )(*args)


def sums_body(x_any, cluster_any, out_ref, low_ref, high_ref, x_ref, cluster_ref, sems):
    copies = [
        pltpu.make_async_copy(cluster_any, cluster_ref, sems.at[0]),
        pltpu.make_async_copy(x_any, x_ref, sems.at[1]),
    ]
    for copy in copies:
        copy.start()
    for copy in copies:
        copy.wait()
    member = (cluster_ref[...] == iota((SUP, NODES), 0)).astype(F32)
    sums = mm(member.astype(BF), x_ref[...])
    counts = jnp.sum(member, 1, keepdims=True)
    diagonal = iota((SUP, WIDTH), 0) == iota((SUP, WIDTH), 1)
    count_row = jnp.sum(jnp.where(diagonal, counts, 0.0), 0, keepdims=True)
    out_ref[:SUP] = sums
    out_ref[SUP:] = jnp.broadcast_to(count_row, (SUM_ROWS - SUP, WIDTH))
    low_ref[...] = x_ref[:HALO]
    high_ref[...] = x_ref[NODES - HALO :]


def chip_sums_body(parts_ref, out_ref):
    total = (parts_ref[0] + parts_ref[1]).astype(BF)
    for peer in range(out_ref.shape[0]):
        out_ref[peer] = total


def near_body(
    low_ref, x_ref, high_ref, grad_ref, slots_ref, links_ref, core_ref, wq_ref, wk_ref, wv_ref, wo_ref,
    qt_ref, at_ref, xt_ref, wt_ref, out_t_ref, gq_t_ref, wkv_ref, base_ref, allowed_ref, inner_ref, outer_ref,
    q_lanes, a_lanes, q_rows, a_rows, weight_all, score_all,
):
    ext = jnp.concatenate([low_ref[...], x_ref[...], high_ref[...]], 0)
    wk = wk_ref[...]
    wv = wv_ref[...]
    queries = mm(x_ref[...], wq_ref[...]).astype(BF)
    keys = mm(ext, wk).astype(BF)
    vals = mm(ext, wv).astype(BF)
    grad_attn = mm_nt(grad_ref[...], wo_ref[...]).astype(BF)
    q_t = flip(queries)
    a_t = flip(grad_attn)
    keys_t = flip(keys)
    vals_t = flip(vals)
    qt_ref[...] = q_t
    at_ref[...] = a_t
    stack_lanes(q_lanes, q_t)
    stack_lanes(a_lanes, a_t)
    stack_rows(q_rows, queries)
    stack_rows(a_rows, grad_attn)
    slots = slots_ref[...]
    row = iota((EXT, NODES), 0)
    count = jnp.zeros((EXT, NODES), F32)
    for j in range(slots.shape[0]):
        count = count + jnp.where(slots[j : j + 1] == row, 1.0, 0.0)
    log_count = jnp.where(count > 0.0, jnp.log(jnp.maximum(count, 1.0)), NEVER)
    for h in range(HEADS):
        score = mm(keys, q_lanes[:, lanes_of(h)])
        e = jnp.exp(score * SCORE_SCALE + log_count)
        prob = e * (1.0 / jnp.sum(e, 0, keepdims=True))
        weight = prob.astype(BF)
        g = mm(vals, a_lanes[:, lanes_of(h)])
        centre = jnp.sum(prob * g, 0, keepdims=True)
        d_score = (prob * (g - centre) * SCORE_SCALE).astype(BF)
        weight_all[:, lanes_of(h)] = weight
        score_all[:, lanes_of(h)] = d_score
        out_t_ref[rows_of(h)] = mm(vals_t[rows_of(h)], weight)
        gq_t_ref[rows_of(h)] = mm(keys_t[rows_of(h)], d_score)
    grad_keys = mm(score_all[...], q_rows[...]).astype(BF)
    grad_vals = mm(weight_all[...], a_rows[...]).astype(BF)
    ext_t = flip(ext)
    xt_ref[...] = ext_t[:, HALO : HALO + NODES]
    wt_ref[:WIDTH] = flip(wq_ref[...])
    wt_ref[WIDTH : 2 * WIDTH] = flip(wk)
    wt_ref[2 * WIDTH :] = flip(wv)
    wkv_ref[0] = mm(ext_t, grad_keys)
    wkv_ref[1] = mm(ext_t, grad_vals)
    back = mm_nt(grad_keys, wk) + mm_nt(grad_vals, wv)
    base_ref[...] = grad_ref[...].astype(F32) + back[HALO : HALO + NODES]
    below, above = back[:HALO], back[HALO + NODES :]
    first = jnp.broadcast_to(core_ref[0], below.shape) == 0
    inner_ref[...] = jnp.where(first, above, below).astype(BF)
    outer_ref[...] = jnp.where(first, below, above).astype(BF)
    links = links_ref[...]
    target = iota((SUP, SUP), 0)
    linked = links[:1] == target
    for l in range(1, links.shape[0]):
        linked = jnp.logical_or(linked, links[l : l + 1] == target)
    allowed_ref[...] = jnp.where(linked, 0.0, NEVER)


def softmax_rows(scores):
    e = jnp.exp(scores)
    return e * (1.0 / jnp.sum(e, 0, keepdims=True))


def score_grad(prob, g):
    return (prob * (g - jnp.sum(prob * g, 0, keepdims=True)) * SCORE_SCALE).astype(BF)


def far_body(
    parts_ref, allowed_ref, grad_ref, wq_ref, wk_ref, wv_ref, wt_ref,
    qt_ref, at_ref, xt_ref, near_t_ref, near_gq_ref, wkv_ref, inner_ref, core_ref,
    mine_ref, mine_pooled_ref, theirs_ref, gq_t_ref,
):
    heads = [rows_of(h) for h in range(HEADS)]
    wq = wq_ref[...]
    wk = wk_ref[...]
    wv = wv_ref[...]
    wt = wt_ref[...]
    totals = jnp.sum(parts_ref[...].astype(F32), 0)
    diagonal = iota((SUP, WIDTH), 0) == iota((SUP, WIDTH), 1)
    counts = jnp.sum(jnp.where(diagonal, totals[SUP : SUP + 1], 0.0), 1, keepdims=True)
    inverse = 1.0 / jnp.maximum(counts, 1.0)
    pooled = (totals[:SUP] * inverse).astype(BF)
    pooled_t = flip(pooled)

    s_proj_t = mm(wt, pooled_t).astype(BF)
    s_qt, s_kt, s_vt = (s_proj_t[i * WIDTH : (i + 1) * WIDTH] for i in range(3))
    s_k = mm(pooled, wk).astype(BF)
    s_v = mm(pooled, wv).astype(BF)
    allowed = allowed_ref[...]
    s_prob = [softmax_rows(mm(s_k[:, h], s_qt[h]) * SCORE_SCALE + allowed) for h in heads]
    s_weight = [p.astype(BF) for p in s_prob]
    moved_t = jnp.concatenate([mm(s_vt[h], w) for h, w in zip(heads, s_weight)], 0)
    state_t = (pooled_t.astype(F32) + moved_t).astype(BF)
    state = flip(state_t)

    c_proj_t = mm(wt[WIDTH:], state_t).astype(BF)
    c_kt, c_vt = c_proj_t[:WIDTH], c_proj_t[WIDTH:]
    c_k = mm(state, wk).astype(BF)
    c_v = mm(state, wv).astype(BF)
    q_t = qt_ref[...]
    a_t = at_ref[...]
    out_t = []
    gq_t = []
    gck_t = []
    gcv_t = []
    for h in heads:
        prob = softmax_rows(mm(c_k[:, h], q_t[h]) * SCORE_SCALE)
        weight = prob.astype(BF)
        d_score = score_grad(prob, mm(c_v[:, h], a_t[h]))
        out_t.append(mm(c_vt[h], weight))
        gq_t.append(mm(c_kt[h], d_score))
        gck_t.append(mm_nt(q_t[h], d_score))
        gcv_t.append(mm_nt(a_t[h], weight))
    gck_t = jnp.concatenate(gck_t, 0).astype(BF)
    gcv_t = jnp.concatenate(gcv_t, 0).astype(BF)

    grad_state_t = mm(jnp.concatenate([wk, wv], 1), jnp.concatenate([gck_t, gcv_t], 0))
    gs_t = grad_state_t.astype(BF)
    gsq_t = []
    gsk_t = []
    gsv_t = []
    for h, prob, weight in zip(heads, s_prob, s_weight):
        d_score = score_grad(prob, mm(s_v[:, h], gs_t[h]))
        gsq_t.append(mm(s_kt[h], d_score))
        gsk_t.append(mm_nt(s_qt[h], d_score))
        gsv_t.append(mm_nt(gs_t[h], weight))
    gsq_t = jnp.concatenate(gsq_t, 0).astype(BF)
    gsk_t = jnp.concatenate(gsk_t, 0).astype(BF)
    gsv_t = jnp.concatenate(gsv_t, 0).astype(BF)
    grad_pooled_t = grad_state_t + mm(
        jnp.concatenate([wq, wk, wv], 1), jnp.concatenate([gsq_t, gsk_t, gsv_t], 0)
    )
    share = grad_pooled_t.T * inverse

    gq_t = (near_gq_ref[...] + jnp.concatenate(gq_t, 0)).astype(BF)
    gq_t_ref[...] = gq_t
    attended_t = (near_t_ref[...] + jnp.concatenate(out_t, 0)).astype(BF)
    grads = [
        mm_nt(xt_ref[...], gq_t) + mm_nt(pooled_t, gsq_t),
        wkv_ref[0] + mm_nt(jnp.concatenate([pooled_t, state_t], 1), jnp.concatenate([gsk_t, gck_t], 1)),
        wkv_ref[1] + mm_nt(jnp.concatenate([pooled_t, state_t], 1), jnp.concatenate([gsv_t, gcv_t], 1)),
        mm(attended_t, grad_ref[...]),
    ]
    core = core_ref[0]
    groups = mine_ref.shape[1]
    rows = mine_ref.shape[2]
    first = jnp.broadcast_to(core, (groups, rows, WIDTH)) == 0
    for w in range(4):
        pairs = grads[w].reshape(groups, 2, rows, WIDTH)
        low, high = pairs[:, 0], pairs[:, 1]
        mine_ref[w] = jnp.where(first, low, high)
        theirs_ref[w * groups * rows : (w + 1) * groups * rows] = (
            jnp.where(first, high, low).reshape(groups * rows, WIDTH).astype(BF)
        )
    half = SUP // 2
    first = jnp.broadcast_to(core, (half, WIDTH)) == 0
    mine_pooled_ref[...] = jnp.where(first, share[:half], share[half:])
    end = 4 * groups * rows + half
    theirs_ref[4 * groups * rows : end] = jnp.where(first, share[half:], share[:half]).astype(BF)
    theirs_ref[end:] = inner_ref[...]


def own_body(base_ref, gq_t_ref, wq_ref, inner_ref, outer_ref, core_ref, out_ref):
    own = base_ref[...] + mm_nt(flip(gq_t_ref[...]), wq_ref[...])
    inner, outer = inner_ref[...].astype(F32), outer_ref[...].astype(F32)
    first = jnp.broadcast_to(core_ref[0], inner.shape) == 0
    out_ref[:HALO] = own[:HALO] + jnp.where(first, outer, inner)
    out_ref[HALO : NODES - HALO] = own[HALO : NODES - HALO]
    out_ref[NODES - HALO :] = own[NODES - HALO :] + jnp.where(first, inner, outer)


def chip_grads_body(mine_ref, mine_pooled_ref, both_ref, core_ref, out_ref, inner_ref):
    received = both_ref[1 - core_ref[0]].astype(F32)
    n_w, n_z, rows, _ = mine_ref.shape
    size = n_w * n_z * rows
    weights = mine_ref[...] + received[:size].reshape(mine_ref.shape)
    pooled = mine_pooled_ref[...] + received[size : size + mine_pooled_ref.shape[0]]
    inner_ref[...] = received[size + mine_pooled_ref.shape[0] :].astype(BF)
    quarter = pooled.shape[0] // n_w
    for w in range(n_w):
        piece = pooled[w * quarter : (w + 1) * quarter]
        for z in range(n_z):
            out_ref[w * n_z + z] = jnp.concatenate([weights[w, z], piece], 0).astype(BF)


def shares_body(n_w, pieces_ref, own_ref, out_ref, pooled_ref):
    n_z = pieces_ref.shape[0] // n_w
    sums = [jnp.sum(pieces_ref[w * n_z : (w + 1) * n_z].astype(F32), 0) for w in range(n_w)]
    rows = out_ref.shape[1]
    share = sum(part[:rows] for part in sums).astype(BF)
    for y in range(out_ref.shape[0]):
        out_ref[y] = share
    pooled_ref[...] = jnp.concatenate([part[rows:] for part in sums], 0).astype(BF)


def columns_body(parts_ref, pooled_ref, out_ref):
    share = jnp.sum(parts_ref[...].astype(F32), 0)
    pooled = pooled_ref[...].astype(F32)
    n_w = out_ref.shape[0]
    quarter = pooled.shape[1] // n_w
    for w in range(n_w):
        rows = slice(w * quarter, (w + 1) * quarter)
        out_ref[w] = jnp.concatenate([share, pooled[0, rows], pooled[1, rows]], 0).astype(BF)


def final_body(scale, parts_ref, own_ref, cluster_ref, weights_ref, nodes_ref):
    n_w, rows, _ = weights_ref.shape
    quarter = (parts_ref.shape[1] - rows) // 2
    parts = parts_ref[...].astype(F32)
    weights_ref[...] = parts[:, :rows] * scale
    halves = [parts[w, rows + c * quarter : rows + (c + 1) * quarter] for c in range(2) for w in range(n_w)]
    pooled = jnp.concatenate(halves, 0).astype(BF)
    member = (cluster_ref[...] == iota((SUP, NODES), 0)).astype(F32).T.astype(BF)
    nodes_ref[...] = (own_ref[...] + mm(member, pooled)).astype(BF)


def swap(parts, axes):
    return lax.all_to_all(parts, axes, 0, 0, tiled=True)


def local(sizes, node_feats, grad_out, neighbours, cluster, super_links, w_query, w_key, w_value, w_out):
    n_x, n_y, n_z, n_c = sizes
    n_super = n_z * n_c
    n_dom = n_x * n_y
    supers = ("z", "c")
    up = [(i, (i + 1) % n_super) for i in range(n_super)]
    down = [(i, (i + n_super - 1) % n_super) for i in range(n_super)]
    cluster_row = cluster.reshape(1, NODES)
    sums, first_rows, last_rows = call(
        sums_body,
        "cluster_sums",
        [((SUM_ROWS, WIDTH), F32), ((HALO, WIDTH), BF), ((HALO, WIDTH), BF)],
        [((NODES, WIDTH), BF), ((1, NODES), jnp.int32), pltpu.SemaphoreType.DMA((2,))],
        1 << 22,
        node_feats, cluster_row,
        outside=(0, 1),
    )
    (sums,) = call(
        chip_sums_body, "chip_sums", [((n_z, SUM_ROWS, WIDTH), BF)], [], 1 << 20, lax.all_gather(sums, "c")
    )
    core = lax.axis_index("c").reshape(1)
    low = lax.ppermute(last_rows, supers, up)
    high = lax.ppermute(first_rows, supers, down)
    parts = swap(sums, "z")
    q_t, a_t, x_t, w_t, near_t, near_gq, wkv, base, allowed, inner, outer = call(
        near_body,
        "near_attention",
        [
            ((WIDTH, NODES), BF), ((WIDTH, NODES), BF), ((WIDTH, NODES), BF), ((3 * WIDTH, WIDTH), BF),
            ((WIDTH, NODES), F32), ((WIDTH, NODES), F32), ((2, WIDTH, WIDTH), F32), ((NODES, WIDTH), F32),
            ((SUP, SUP), F32), ((HALO, WIDTH), BF), ((HALO, WIDTH), BF),
        ],
        [
            ((WIDTH, STACK), BF), ((WIDTH, STACK), BF), ((STACK, WIDTH), BF), ((STACK, WIDTH), BF),
            ((EXT, STACK), BF), ((EXT, STACK), BF),
        ],
        10 << 30,
        low, node_feats, high, grad_out, neighbours.T, super_links.T, core, w_query, w_key, w_value, w_out,
    )
    outward = [(2 * z, (2 * z - 1) % n_super) for z in range(n_z)]
    outward += [(2 * z + 1, (2 * z + 2) % n_super) for z in range(n_z)]
    outer = lax.ppermute(outer, supers, outward)
    share_rows = WIDTH // n_super
    weight_rows = 4 * n_z * share_rows
    half = (SUP // 2, WIDTH)
    mine, mine_pooled, theirs, gq_t = call(
        far_body,
        "far_attention",
        [
            ((4, n_z, share_rows, WIDTH), F32), (half, F32), ((weight_rows + SUP // 2 + HALO, WIDTH), BF),
            ((WIDTH, NODES), BF),
        ],
        [],
        10 << 30,
        parts, allowed, grad_out, w_query, w_key, w_value, w_t,
        q_t, a_t, x_t, near_t, near_gq, wkv, inner, core,
    )
    message_rows = share_rows + SUP // 2 // n_x
    pieces, inner = call(
        chip_grads_body,
        "chip_grads",
        [((n_x * n_z, message_rows, WIDTH), BF), ((HALO, WIDTH), BF)],
        [],
        1 << 20,
        mine, mine_pooled, lax.all_gather(theirs, "c"), core,
    )
    pieces = swap(pieces, ("x", "z"))
    (own,) = call(
        own_body, "own_nodes", [((NODES, WIDTH), F32)], [], 1 << 28, base, gq_t, w_query, inner, outer, core
    )
    shares, pooled = call(
        functools.partial(shares_body, n_x),
        "weight_shares",
        [((n_y, share_rows, WIDTH), BF), (half, BF)],
        [],
        1 << 20,
        pieces, own,
        outside=(1,),
    )
    shares = swap(shares, "y")
    (columns,) = call(
        columns_body,
        "weight_columns",
        [((n_x, message_rows + SUP // 2 // n_x, WIDTH), BF)],
        [],
        1 << 20,
        shares, lax.all_gather(pooled, "c"),
    )
    columns = swap(columns, "x")
    scale = 1.0 / math.sqrt(NODES * n_super * n_dom)
    grad_weights, grad_nodes = call(
        functools.partial(final_body, scale),
        "gradients",
        [((4, share_rows, WIDTH), F32), ((NODES, WIDTH), BF)],
        [],
        1 << 20,
        columns, own, cluster_row,
    )
    return grad_nodes, grad_weights


def solution(mesh):
    n_dom = mesh.shape["dom"]
    n_super = mesh.shape["super"]
    sizes = (4, n_dom // 4, n_super // 2, 2)
    fine = Mesh(mesh.devices.reshape(sizes), ("x", "y", "z", "c"))
    everyone = ("x", "y", "z", "c")
    return jax.shard_map(
        functools.partial(local, sizes),
        mesh=fine,
        in_specs=(
            P(everyone, None),
            P(everyone, None),
            P(everyone, None),
            P(everyone),
            P(("x", "y"), None),
            P(),
            P(),
            P(),
            P(),
        ),
        out_specs=(P(everyone, None), P(None, ("z", "c"), None)),
        check_vma=False,
    )
```

```python
import functools
import math

import jax
import jax.numpy as jnp
from jax import lax
from jax.experimental import pallas as pl
from jax.experimental.pallas import tpu as pltpu
from jax.sharding import Mesh, PartitionSpec as P

WIDTH = 256
HEADS = 8
HEAD_DIM = 32
NODES = 128
HALO = 32
EXT = NODES + 2 * HALO
SUP = 64
SUM_ROWS = SUP + 8
STACK = HEADS * NODES
CHIP_ROWS = (256, 256, 128, 128, 256, 256, 512, 64)
CHIP_AT = tuple(sum(CHIP_ROWS[:i]) for i in range(len(CHIP_ROWS) + 1))
SCORE_SCALE = 1.0 / math.sqrt(HEAD_DIM)
NEVER = -1e30
BF = jnp.bfloat16
F32 = jnp.float32


def mm(a, b):
    return jnp.dot(a, b, preferred_element_type=F32)


def mm_nt(a, b):
    return lax.dot_general(a, b, (((1,), (1,)), ((), ())), preferred_element_type=F32)


def iota(shape, dim):
    return lax.broadcasted_iota(jnp.int32, shape, dim)


def flip(a):
    return a.astype(F32).T.astype(a.dtype)


def rows_of(h):
    return slice(h * HEAD_DIM, (h + 1) * HEAD_DIM)


def lanes_of(h):
    return slice(h * NODES, (h + 1) * NODES)


def split_rows(m, core):
    pairs = m.reshape(m.shape[0] // 32, 2, 16, m.shape[1])
    low, high = pairs[:, 0], pairs[:, 1]
    first = jnp.broadcast_to(core, low.shape) == 0
    shape = (m.shape[0] // 2, m.shape[1])
    return jnp.where(first, low, high).reshape(shape), jnp.where(first, high, low).reshape(shape)


def stack_lanes(ref, flipped):
    ref[...] = jnp.zeros(ref.shape, ref.dtype)
    for h in range(HEADS):
        ref[rows_of(h), lanes_of(h)] = flipped[rows_of(h)]


def stack_rows(ref, rows):
    head = lax.shift_right_logical(iota(rows.shape, 1), 5)
    wide = rows.astype(F32)
    for h in range(HEADS):
        ref[lanes_of(h), :] = jnp.where(head == h, wide, 0.0).astype(rows.dtype)


def call(body, name, outs, scratch, flops, *args, outside=()):
    size = sum(a.size * a.dtype.itemsize for a in args)
    vmem = pl.BlockSpec(memory_space=pltpu.VMEM)
    smem = pl.BlockSpec(memory_space=pltpu.SMEM)
    anywhere = pl.BlockSpec(memory_space=pltpu.HBM)
    return pl.pallas_call(
        body,
        in_specs=[anywhere if i in outside else smem if a.ndim == 1 else vmem for i, a in enumerate(args)],
        name=name,
        out_shape=tuple(jax.ShapeDtypeStruct(s, d) for s, d in outs),
        scratch_shapes=[pltpu.VMEM(*s) if isinstance(s, tuple) else s for s in scratch],
        compiler_params=pltpu.CompilerParams(vmem_limit_bytes=32 * 1024 * 1024),
        cost_estimate=pl.CostEstimate(flops=flops, bytes_accessed=size, transcendentals=0),
    )(*args)


def sums_body(x_any, cluster_any, out_ref, low_ref, high_ref, x_ref, cluster_ref, sems):
    copies = [
        pltpu.make_async_copy(cluster_any, cluster_ref, sems.at[0]),
        pltpu.make_async_copy(x_any, x_ref, sems.at[1]),
    ]
    for copy in copies:
        copy.start()
    for copy in copies:
        copy.wait()
    member = (cluster_ref[...] == iota((SUP, NODES), 0)).astype(F32)
    sums = mm(member.astype(BF), x_ref[...])
    counts = jnp.sum(member, 1, keepdims=True)
    diagonal = iota((SUP, WIDTH), 0) == iota((SUP, WIDTH), 1)
    count_row = jnp.sum(jnp.where(diagonal, counts, 0.0), 0, keepdims=True)
    out_ref[:SUP] = sums
    out_ref[SUP:] = jnp.broadcast_to(count_row, (SUM_ROWS - SUP, WIDTH))
    low_ref[...] = x_ref[:HALO]
    high_ref[...] = x_ref[NODES - HALO :]


def chip_sums_body(parts_ref, out_ref):
    total = (parts_ref[0] + parts_ref[1]).astype(BF)
    for peer in range(out_ref.shape[0]):
        out_ref[peer] = total


def near_body(
    low_ref, x_ref, high_ref, grad_ref, slots_ref, links_ref, core_ref, wq_ref, wk_ref, wv_ref, wo_ref,
    qt_ref, at_ref, xt_ref, wt_ref, out_t_ref, gq_t_ref, wkv_ref, base_ref, allowed_ref, chip_ref, outer_ref,
    q_lanes, a_lanes, q_rows, a_rows, weight_all, score_all, near_t,
):
    ext = jnp.concatenate([low_ref[...], x_ref[...], high_ref[...]], 0)
    wk = wk_ref[...]
    wv = wv_ref[...]
    queries = mm(x_ref[...], wq_ref[...]).astype(BF)
    keys = mm(ext, wk).astype(BF)
    vals = mm(ext, wv).astype(BF)
    grad_attn = mm_nt(grad_ref[...], wo_ref[...]).astype(BF)
    q_t = flip(queries)
    a_t = flip(grad_attn)
    keys_t = flip(keys)
    vals_t = flip(vals)
    qt_ref[...] = q_t
    at_ref[...] = a_t
    stack_lanes(q_lanes, q_t)
    stack_lanes(a_lanes, a_t)
    stack_rows(q_rows, queries)
    stack_rows(a_rows, grad_attn)
    slots = slots_ref[...]
    row = iota((EXT, NODES), 0)
    count = jnp.zeros((EXT, NODES), F32)
    for j in range(slots.shape[0]):
        count = count + jnp.where(slots[j : j + 1] == row, 1.0, 0.0)
    log_count = jnp.where(count > 0.0, jnp.log(jnp.maximum(count, 1.0)), NEVER)
    for h in range(HEADS):
        score = mm(keys, q_lanes[:, lanes_of(h)])
        e = jnp.exp(score * SCORE_SCALE + log_count)
        prob = e * (1.0 / jnp.sum(e, 0, keepdims=True))
        weight = prob.astype(BF)
        g = mm(vals, a_lanes[:, lanes_of(h)])
        centre = jnp.sum(prob * g, 0, keepdims=True)
        d_score = (prob * (g - centre) * SCORE_SCALE).astype(BF)
        weight_all[:, lanes_of(h)] = weight
        score_all[:, lanes_of(h)] = d_score
        near_t[rows_of(h)] = mm(vals_t[rows_of(h)], weight)
        gq_t_ref[rows_of(h)] = mm(keys_t[rows_of(h)], d_score)
    grad_keys = mm(score_all[...], q_rows[...]).astype(BF)
    grad_vals = mm(weight_all[...], a_rows[...]).astype(BF)
    core = core_ref[0]
    ext_t = ext.astype(F32).T
    wt_ref[:WIDTH] = flip(wq_ref[...])
    wt_ref[WIDTH : 2 * WIDTH] = flip(wk)
    wt_ref[2 * WIDTH :] = flip(wv)
    x_mine, x_other = split_rows(ext_t[:, HALO : HALO + NODES], core)
    xt_ref[...] = x_mine.astype(BF)
    near_mine, near_other = split_rows(near_t[...], core)
    out_t_ref[...] = near_mine
    ext_t = ext_t.astype(BF)
    key_mine, key_other = split_rows(mm(ext_t, grad_keys), core)
    val_mine, val_other = split_rows(mm(ext_t, grad_vals), core)
    wkv_ref[0] = key_mine
    wkv_ref[1] = val_mine
    chip = [
        q_t, a_t, x_other, near_other, gq_t_ref[...], grad_ref[:, :NODES], grad_ref[:, NODES:],
        key_other[:, :NODES], key_other[:, NODES:], val_other[:, :NODES], val_other[:, NODES:],
    ]
    at = 0
    for part in chip:
        chip_ref[at : at + part.shape[0]] = part.astype(BF)
        at += part.shape[0]
    back = mm_nt(grad_keys, wk) + mm_nt(grad_vals, wv)
    base_ref[...] = grad_ref[...].astype(F32) + back[HALO : HALO + NODES]
    below, above = back[:HALO], back[HALO + NODES :]
    first = jnp.broadcast_to(core, below.shape) == 0
    inner = jnp.where(first, above, below).astype(BF)
    chip_ref[at : at + HALO] = inner[:, :NODES]
    chip_ref[at + HALO :] = inner[:, NODES:]
    outer_ref[...] = jnp.where(first, below, above).astype(BF)
    links = links_ref[...]
    target = iota((SUP, SUP), 0)
    linked = links[:1] == target
    for l in range(1, links.shape[0]):
        linked = jnp.logical_or(linked, links[l : l + 1] == target)
    allowed_ref[...] = jnp.where(linked, 0.0, NEVER)


def softmax_rows(scores):
    e = jnp.exp(scores)
    return e * (1.0 / jnp.sum(e, 0, keepdims=True))


def score_grad(prob, g):
    return (prob * (g - jnp.sum(prob * g, 0, keepdims=True)) * SCORE_SCALE).astype(BF)


def far_body(
    parts_ref, allowed_ref, both_ref, grad_ref, wq_ref, wk_ref, wv_ref, wt_ref,
    qt_ref, at_ref, xt_ref, near_t_ref, near_gq_ref, wkv_ref, core_ref,
    message_ref, gq_t_ref, inner_ref,
):
    core = core_ref[0]
    sibling = both_ref.at[1 - core]

    def section(i):
        return sibling[CHIP_AT[i] : CHIP_AT[i + 1]]

    def folded(i):
        rows = section(i)
        half = rows.shape[0] // 2
        return jnp.concatenate([rows[:half], rows[half:]], 1)

    heads = [rows_of(h) for h in range(HEADS)]
    wq = wq_ref[...]
    wk = wk_ref[...]
    wv = wv_ref[...]
    wt = wt_ref[...]
    totals = jnp.sum(parts_ref[...].astype(F32), 0)
    diagonal = iota((SUP, WIDTH), 0) == iota((SUP, WIDTH), 1)
    counts = jnp.sum(jnp.where(diagonal, totals[SUP : SUP + 1], 0.0), 1, keepdims=True)
    inverse = 1.0 / jnp.maximum(counts, 1.0)
    pooled = (totals[:SUP] * inverse).astype(BF)
    pooled_t = flip(pooled)

    s_proj_t = mm(wt, pooled_t).astype(BF)
    s_qt, s_kt, s_vt = (s_proj_t[i * WIDTH : (i + 1) * WIDTH] for i in range(3))
    s_k = mm(pooled, wk).astype(BF)
    s_v = mm(pooled, wv).astype(BF)
    allowed = allowed_ref[...]
    s_prob = [softmax_rows(mm(s_k[:, h], s_qt[h]) * SCORE_SCALE + allowed) for h in heads]
    s_weight = [p.astype(BF) for p in s_prob]
    moved_t = jnp.concatenate([mm(s_vt[h], w) for h, w in zip(heads, s_weight)], 0)
    state_t = pooled_t.astype(F32) + moved_t
    low_rank = jnp.concatenate(
        [split_rows(pooled_t.astype(F32), core)[0], split_rows(state_t, core)[0]], 1
    ).astype(BF)
    state_t = state_t.astype(BF)
    state = flip(state_t)

    c_proj_t = mm(wt[WIDTH:], state_t)
    c_kt = c_proj_t[:WIDTH].astype(BF)
    c_vt = split_rows(c_proj_t[WIDTH:], core)[0].astype(BF)
    c_k = mm(state, wk).astype(BF)
    c_v = mm(state, wv).astype(BF)
    q_t = jnp.concatenate([qt_ref[...], section(0)], 1)
    a_t = jnp.concatenate([at_ref[...], section(1)], 1)
    out_t = []
    gq_t = []
    gck_t = []
    gcv_t = []
    for i, h in enumerate(heads):
        prob = softmax_rows(mm(c_k[:, h], q_t[h]) * SCORE_SCALE)
        weight = prob.astype(BF)
        d_score = score_grad(prob, mm(c_v[:, h], a_t[h]))
        out_t.append(mm(c_vt[i * 16 : (i + 1) * 16], weight))
        gq_t.append(mm(c_kt[h], d_score))
        gck_t.append(mm_nt(q_t[h], d_score))
        gcv_t.append(mm_nt(a_t[h], weight))
    gck_t = jnp.concatenate(gck_t, 0).astype(BF)
    gcv_t = jnp.concatenate(gcv_t, 0).astype(BF)

    grad_state_t = mm(jnp.concatenate([wk, wv], 1), jnp.concatenate([gck_t, gcv_t], 0))
    gs_t = grad_state_t.astype(BF)
    gsq_t = []
    gsk_t = []
    gsv_t = []
    for h, prob, weight in zip(heads, s_prob, s_weight):
        d_score = score_grad(prob, mm(s_v[:, h], gs_t[h]))
        gsq_t.append(mm(s_kt[h], d_score))
        gsk_t.append(mm_nt(s_qt[h], d_score))
        gsv_t.append(mm_nt(gs_t[h], weight))
    gsq_t = jnp.concatenate(gsq_t, 0).astype(BF)
    gsk_t = jnp.concatenate(gsk_t, 0).astype(BF)
    gsv_t = jnp.concatenate(gsv_t, 0).astype(BF)
    grad_pooled_t = grad_state_t + mm(
        jnp.concatenate([wq, wk, wv], 1), jnp.concatenate([gsq_t, gsk_t, gsv_t], 0)
    )
    share = grad_pooled_t.T * inverse

    near_gq = jnp.concatenate([near_gq_ref[...], section(4).astype(F32)], 1)
    gq_t = (near_gq + jnp.concatenate(gq_t, 0)).astype(BF)
    gq_t_ref[...] = gq_t[:, :NODES]
    near_t = jnp.concatenate([near_t_ref[...], section(3).astype(F32)], 1)
    attended_t = (near_t + jnp.concatenate(out_t, 0)).astype(BF)
    x_t = jnp.concatenate([xt_ref[...], section(2)], 1)
    grad_out = jnp.concatenate([grad_ref[...], folded(5)], 0)
    near_kv = section(6).astype(F32)
    rows = near_kv.shape[0] // 4
    near_k = wkv_ref[0] + jnp.concatenate([near_kv[:rows], near_kv[rows : 2 * rows]], 1)
    near_v = wkv_ref[1] + jnp.concatenate([near_kv[2 * rows : 3 * rows], near_kv[3 * rows :]], 1)
    inner_ref[...] = folded(7)
    grads = [
        mm_nt(jnp.concatenate([x_t, low_rank[:, :SUP]], 1), jnp.concatenate([gq_t, gsq_t], 1)),
        near_k + mm_nt(low_rank, jnp.concatenate([gsk_t, gck_t], 1)),
        near_v + mm_nt(low_rank, jnp.concatenate([gsv_t, gcv_t], 1)),
        mm(attended_t, grad_out),
    ]
    half = SUP // 2
    first = jnp.broadcast_to(core, (half, WIDTH)) == 0
    pooled_half = jnp.where(first, share[:half], share[half:])
    quarter = half // len(grads)
    message_rows = message_ref.shape[1]
    n_z = message_ref.shape[0] // len(grads)
    own_rows = message_rows - quarter
    for w, grad in enumerate(grads):
        piece = pooled_half[w * quarter : (w + 1) * quarter]
        for z in range(n_z):
            rows = grad[z * own_rows : (z + 1) * own_rows]
            message_ref[w * n_z + z] = jnp.concatenate([rows, piece], 0).astype(BF)


def own_body(base_ref, gq_t_ref, wq_ref, inner_ref, outer_ref, core_ref, out_ref):
    own = base_ref[...] + mm_nt(flip(gq_t_ref[...]), wq_ref[...])
    inner, outer = inner_ref[...].astype(F32), outer_ref[...].astype(F32)
    first = jnp.broadcast_to(core_ref[0], inner.shape) == 0
    out_ref[:HALO] = own[:HALO] + jnp.where(first, outer, inner)
    out_ref[HALO : NODES - HALO] = own[HALO : NODES - HALO]
    out_ref[NODES - HALO :] = own[NODES - HALO :] + jnp.where(first, inner, outer)


def shares_body(n_w, pieces_ref, own_ref, out_ref, pooled_ref):
    n_z = pieces_ref.shape[0] // n_w
    sums = [jnp.sum(pieces_ref[w * n_z : (w + 1) * n_z].astype(F32), 0) for w in range(n_w)]
    rows = out_ref.shape[1]
    share = sum(part[:rows] for part in sums).astype(BF)
    for y in range(out_ref.shape[0]):
        out_ref[y] = share
    pooled_ref[...] = jnp.concatenate([part[rows:] for part in sums], 0).astype(BF)


def columns_body(parts_ref, pooled_ref, out_ref):
    share = jnp.sum(parts_ref[...].astype(F32), 0)
    pooled = pooled_ref[...].astype(F32)
    n_w = out_ref.shape[0]
    quarter = pooled.shape[1] // n_w
    for w in range(n_w):
        rows = slice(w * quarter, (w + 1) * quarter)
        out_ref[w] = jnp.concatenate([share, pooled[0, rows], pooled[1, rows]], 0).astype(BF)


def final_body(scale, parts_ref, own_ref, cluster_ref, weights_ref, nodes_ref):
    n_w, rows, _ = weights_ref.shape
    quarter = (parts_ref.shape[1] - rows) // 2
    parts = parts_ref[...].astype(F32)
    weights_ref[...] = parts[:, :rows] * scale
    halves = [parts[w, rows + c * quarter : rows + (c + 1) * quarter] for c in range(2) for w in range(n_w)]
    pooled = jnp.concatenate(halves, 0).astype(BF)
    member = (cluster_ref[...] == iota((SUP, NODES), 0)).astype(F32).T.astype(BF)
    nodes_ref[...] = (own_ref[...] + mm(member, pooled)).astype(BF)


def swap(parts, axes):
    return lax.all_to_all(parts, axes, 0, 0, tiled=True)


def local(sizes, node_feats, grad_out, neighbours, cluster, super_links, w_query, w_key, w_value, w_out):
    n_x, n_y, n_z, n_c = sizes
    n_super = n_z * n_c
    n_dom = n_x * n_y
    supers = ("z", "c")
    up = [(i, (i + 1) % n_super) for i in range(n_super)]
    down = [(i, (i + n_super - 1) % n_super) for i in range(n_super)]
    cluster_row = cluster.reshape(1, NODES)
    sums, first_rows, last_rows = call(
        sums_body,
        "cluster_sums",
        [((SUM_ROWS, WIDTH), F32), ((HALO, WIDTH), BF), ((HALO, WIDTH), BF)],
        [((NODES, WIDTH), BF), ((1, NODES), jnp.int32), pltpu.SemaphoreType.DMA((2,))],
        1 << 22,
        node_feats, cluster_row,
        outside=(0, 1),
    )
    (sums,) = call(
        chip_sums_body, "chip_sums", [((n_z, SUM_ROWS, WIDTH), BF)], [], 1 << 20, lax.all_gather(sums, "c")
    )
    core = lax.axis_index("c").reshape(1)
    low = lax.ppermute(last_rows, supers, up)
    high = lax.ppermute(first_rows, supers, down)
    parts = swap(sums, "z")
    q_t, a_t, x_t, w_t, near_t, near_gq, wkv, base, allowed, chip, outer = call(
        near_body,
        "near_attention",
        [
            ((WIDTH, NODES), BF), ((WIDTH, NODES), BF), ((WIDTH // 2, NODES), BF), ((3 * WIDTH, WIDTH), BF),
            ((WIDTH // 2, NODES), F32), ((WIDTH, NODES), F32), ((2, WIDTH // 2, WIDTH), F32), ((NODES, WIDTH), F32),
            ((SUP, SUP), F32), ((CHIP_AT[-1], NODES), BF), ((HALO, WIDTH), BF),
        ],
        [
            ((WIDTH, STACK), BF), ((WIDTH, STACK), BF), ((STACK, WIDTH), BF), ((STACK, WIDTH), BF),
            ((EXT, STACK), BF), ((EXT, STACK), BF), ((WIDTH, NODES), F32),
        ],
        10 << 30,
        low, node_feats, high, grad_out, neighbours.T, super_links.T, core, w_query, w_key, w_value, w_out,
    )
    outward = [(2 * z, (2 * z - 1) % n_super) for z in range(n_z)]
    outward += [(2 * z + 1, (2 * z + 2) % n_super) for z in range(n_z)]
    outer = lax.ppermute(outer, supers, outward)
    share_rows = WIDTH // n_super
    half = (SUP // 2, WIDTH)
    message_rows = share_rows + SUP // 2 // n_x
    pieces, gq_t, inner = call(
        far_body,
        "far_attention",
        [((n_x * n_z, message_rows, WIDTH), BF), ((WIDTH, NODES), BF), ((HALO, WIDTH), BF)],
        [],
        10 << 30,
        parts, allowed, lax.all_gather(chip, "c"), grad_out, w_query, w_key, w_value, w_t,
        q_t, a_t, x_t, near_t, near_gq, wkv, core,
    )
    pieces = swap(pieces, ("x", "z"))
    (own,) = call(
        own_body, "own_nodes", [((NODES, WIDTH), F32)], [], 1 << 28, base, gq_t, w_query, inner, outer, core
    )
    shares, pooled = call(
        functools.partial(shares_body, n_x),
        "weight_shares",
        [((n_y, share_rows, WIDTH), BF), (half, BF)],
        [],
        1 << 20,
        pieces, own,
        outside=(1,),
    )
    shares = swap(shares, "y")
    (columns,) = call(
        columns_body,
        "weight_columns",
        [((n_x, message_rows + SUP // 2 // n_x, WIDTH), BF)],
        [],
        1 << 20,
        shares, lax.all_gather(pooled, "c"),
    )
    columns = swap(columns, "x")
    scale = 1.0 / math.sqrt(NODES * n_super * n_dom)
    grad_weights, grad_nodes = call(
        functools.partial(final_body, scale),
        "gradients",
        [((4, share_rows, WIDTH), F32), ((NODES, WIDTH), BF)],
        [],
        1 << 20,
        columns, own, cluster_row,
    )
    return grad_nodes, grad_weights


def solution(mesh):
    n_dom = mesh.shape["dom"]
    n_super = mesh.shape["super"]
    sizes = (4, n_dom // 4, n_super // 2, 2)
    fine = Mesh(mesh.devices.reshape(sizes), ("x", "y", "z", "c"))
    everyone = ("x", "y", "z", "c")
    return jax.shard_map(
        functools.partial(local, sizes),
        mesh=fine,
        in_specs=(
            P(everyone, None),
            P(everyone, None),
            P(everyone, None),
            P(everyone),
            P(("x", "y"), None),
            P(),
            P(),
            P(),
            P(),
        ),
        out_specs=(P(everyone, None), P(None, ("z", "c"), None)),
        check_vma=False,
    )
```

```python
import functools
import math

import jax
import jax.numpy as jnp
from jax import lax
from jax.experimental import pallas as pl
from jax.experimental.pallas import tpu as pltpu
from jax.sharding import Mesh, PartitionSpec as P

WIDTH = 256
HEADS = 8
HEAD_DIM = 32
NODES = 128
HALO = 32
EXT = NODES + 2 * HALO
SUP = 64
K_TOP = 8
SUM_ROWS = SUP + 8
CHIP_ROWS = (256, 256, 128, 128, 256, 256, 512)
CHIP_AT = tuple(sum(CHIP_ROWS[:i]) for i in range(len(CHIP_ROWS) + 1))
SCORE_SCALE = 1.0 / math.sqrt(HEAD_DIM)
NEVER = -1e30
BF = jnp.bfloat16
F32 = jnp.float32


def mm(a, b):
    return jnp.dot(a, b, preferred_element_type=F32)


def mm_nt(a, b):
    return lax.dot_general(a, b, (((1,), (1,)), ((), ())), preferred_element_type=F32)


def iota(shape, dim):
    return lax.broadcasted_iota(jnp.int32, shape, dim)


def flip(a):
    return a.astype(F32).T.astype(a.dtype)


def rows_of(h):
    return slice(h * HEAD_DIM, (h + 1) * HEAD_DIM)


def split_rows(m, core):
    pairs = m.reshape(m.shape[0] // 32, 2, 16, m.shape[1])
    low, high = pairs[:, 0], pairs[:, 1]
    first = jnp.broadcast_to(core, low.shape) == 0
    shape = (m.shape[0] // 2, m.shape[1])
    return jnp.where(first, low, high).reshape(shape), jnp.where(first, high, low).reshape(shape)


def call(body, name, outs, scratch, flops, *args, outside=(), vmem=32):
    size = sum(a.size * a.dtype.itemsize for a in args)
    inside = pl.BlockSpec(memory_space=pltpu.VMEM)
    smem = pl.BlockSpec(memory_space=pltpu.SMEM)
    anywhere = pl.BlockSpec(memory_space=pltpu.HBM)
    return pl.pallas_call(
        body,
        in_specs=[anywhere if i in outside else smem if a.ndim == 1 else inside for i, a in enumerate(args)],
        name=name,
        out_shape=tuple(jax.ShapeDtypeStruct(s, d) for s, d in outs),
        scratch_shapes=[pltpu.VMEM(*s) if isinstance(s, tuple) else s for s in scratch],
        compiler_params=pltpu.CompilerParams(vmem_limit_bytes=vmem * 1024 * 1024),
        cost_estimate=pl.CostEstimate(flops=flops, bytes_accessed=size, transcendentals=0),
    )(*args)


def softmax_rows(scores):
    e = jnp.exp(scores)
    return e * (1.0 / jnp.sum(e, 0, keepdims=True))


def score_grad(prob, g):
    return (prob * (g - jnp.sum(prob * g, 0, keepdims=True)) * SCORE_SCALE).astype(BF)


def sums_body(
    x_any, cluster_any, links_any, out_ref, low_ref, high_ref, allowed_ref, x_ref, cluster_ref, links_ref, sems
):
    copies = [
        pltpu.make_async_copy(cluster_any, cluster_ref, sems.at[0]),
        pltpu.make_async_copy(x_any, x_ref, sems.at[1]),
        pltpu.make_async_copy(links_any, links_ref, sems.at[2]),
    ]
    for copy in copies:
        copy.start()
    for copy in copies:
        copy.wait()
    member = (cluster_ref[...] == iota((SUP, NODES), 0)).astype(F32)
    sums = mm(member.astype(BF), x_ref[...])
    counts = jnp.sum(member, 1, keepdims=True)
    diagonal = iota((SUP, WIDTH), 0) == iota((SUP, WIDTH), 1)
    count_row = jnp.sum(jnp.where(diagonal, counts, 0.0), 0, keepdims=True)
    count_rows = jnp.broadcast_to(count_row, (SUM_ROWS - SUP, WIDTH))
    message = jnp.concatenate([sums, count_rows], 0).astype(BF)
    for peer in range(out_ref.shape[0]):
        out_ref[peer] = message
    low_ref[...] = x_ref[:HALO]
    high_ref[...] = x_ref[NODES - HALO :]
    links = links_ref[...]
    target = iota((SUP, SUP), 0)
    linked = links[:1] == target
    for l in range(1, links.shape[0]):
        linked = jnp.logical_or(linked, links[l : l + 1] == target)
    allowed_ref[...] = jnp.where(linked, 0.0, NEVER)


def near_body(
    low_ref, x_ref, high_ref, grad_ref, slots_ref, core_ref, wq_ref, wk_ref, wv_ref, wo_ref,
    qt_ref, at_ref, xt_ref, wt_ref, out_t_ref, gq_t_ref, wkv_ref, grad_kv_ref, chip_ref,
    near_t,
):
    ext = jnp.concatenate([low_ref[...], x_ref[...], high_ref[...]], 0)
    wk = wk_ref[...]
    wv = wv_ref[...]
    queries = mm(x_ref[...], wq_ref[...]).astype(BF)
    keys = mm(ext, wk).astype(BF)
    vals = mm(ext, wv).astype(BF)
    grad_attn = mm_nt(grad_ref[...], wo_ref[...]).astype(BF)
    q_t = flip(queries)
    a_t = flip(grad_attn)
    keys_t = flip(keys)
    vals_t = flip(vals)
    qt_ref[...] = q_t
    at_ref[...] = a_t
    slots = slots_ref[...]
    row = iota((EXT, NODES), 0)
    count = jnp.zeros((EXT, NODES), F32)
    for j in range(slots.shape[0]):
        count = count + jnp.where(slots[j : j + 1] == row, 1.0, 0.0)
    log_count = jnp.where(count > 0.0, jnp.log(jnp.maximum(count, 1.0)), NEVER)
    gk_t = []
    gv_t = []
    for h in range(HEADS):
        rows = rows_of(h)
        prob = softmax_rows(mm(keys[:, rows], q_t[rows]) * SCORE_SCALE + log_count)
        weight = prob.astype(BF)
        d_score = score_grad(prob, mm(vals[:, rows], a_t[rows]))
        near_t[rows] = mm(vals_t[rows], weight)
        gq_t_ref[rows] = mm(keys_t[rows], d_score)
        gk_t.append(mm_nt(q_t[rows], d_score))
        gv_t.append(mm_nt(a_t[rows], weight))
    gk_t = jnp.concatenate(gk_t, 0).astype(BF)
    gv_t = jnp.concatenate(gv_t, 0).astype(BF)
    grad_kv_ref[:WIDTH] = gk_t
    grad_kv_ref[WIDTH:] = gv_t
    core = core_ref[0]
    ext_t = ext.astype(F32).T
    wt_ref[:WIDTH] = flip(wq_ref[...])
    wt_ref[WIDTH : 2 * WIDTH] = flip(wk)
    wt_ref[2 * WIDTH :] = flip(wv)
    x_mine, x_other = split_rows(ext_t[:, HALO : HALO + NODES], core)
    xt_ref[...] = x_mine.astype(BF)
    near_mine, near_other = split_rows(near_t[...], core)
    out_t_ref[...] = near_mine
    ext_t = ext_t.astype(BF)
    key_mine, key_other = split_rows(mm_nt(ext_t, gk_t), core)
    val_mine, val_other = split_rows(mm_nt(ext_t, gv_t), core)
    wkv_ref[0] = key_mine
    wkv_ref[1] = val_mine
    chip = [
        q_t, a_t, x_other, near_other, gq_t_ref[...], grad_ref[:, :NODES], grad_ref[:, NODES:],
        key_other[:, :NODES], key_other[:, NODES:], val_other[:, :NODES], val_other[:, NODES:],
    ]
    at = 0
    for part in chip:
        chip_ref[at : at + part.shape[0]] = part.astype(BF)
        at += part.shape[0]


def far_body(
    parts_ref, allowed_ref, both_ref, grad_ref, wq_ref, wk_ref, wv_ref, wt_ref,
    qt_ref, at_ref, xt_ref, near_t_ref, near_gq_ref, wkv_ref, core_ref,
    message_ref, gq_t_ref,
):
    core = core_ref[0]
    sibling = both_ref.at[1 - core]

    def section(i):
        return sibling[CHIP_AT[i] : CHIP_AT[i + 1]]

    def folded(i):
        rows = section(i)
        half = rows.shape[0] // 2
        return jnp.concatenate([rows[:half], rows[half:]], 1)

    heads = [rows_of(h) for h in range(HEADS)]
    wq = wq_ref[...]
    wk = wk_ref[...]
    wv = wv_ref[...]
    wt = wt_ref[...]
    totals = jnp.sum(parts_ref[...].astype(F32), 0)
    diagonal = iota((SUP, WIDTH), 0) == iota((SUP, WIDTH), 1)
    counts = jnp.sum(jnp.where(diagonal, totals[SUP : SUP + 1], 0.0), 1, keepdims=True)
    inverse = 1.0 / jnp.maximum(counts, 1.0)
    pooled = (totals[:SUP] * inverse).astype(BF)
    pooled_t = flip(pooled)

    s_proj_t = mm(wt, pooled_t).astype(BF)
    s_qt, s_kt, s_vt = (s_proj_t[i * WIDTH : (i + 1) * WIDTH] for i in range(3))
    s_k = mm(pooled, wk).astype(BF)
    s_v = mm(pooled, wv).astype(BF)
    allowed = allowed_ref[...]
    s_prob = [softmax_rows(mm(s_k[:, h], s_qt[h]) * SCORE_SCALE + allowed) for h in heads]
    s_weight = [p.astype(BF) for p in s_prob]
    moved_t = jnp.concatenate([mm(s_vt[h], w) for h, w in zip(heads, s_weight)], 0)
    state_t = pooled_t.astype(F32) + moved_t
    low_rank = jnp.concatenate(
        [split_rows(pooled_t.astype(F32), core)[0], split_rows(state_t, core)[0]], 1
    ).astype(BF)
    state_t = state_t.astype(BF)
    state = flip(state_t)

    c_proj_t = mm(wt[WIDTH:], state_t)
    c_kt = c_proj_t[:WIDTH].astype(BF)
    c_vt = split_rows(c_proj_t[WIDTH:], core)[0].astype(BF)
    c_k = mm(state, wk).astype(BF)
    c_v = mm(state, wv).astype(BF)
    q_t = jnp.concatenate([qt_ref[...], section(0)], 1)
    a_t = jnp.concatenate([at_ref[...], section(1)], 1)
    out_t = []
    gq_t = []
    gck_t = []
    gcv_t = []
    for i, h in enumerate(heads):
        prob = softmax_rows(mm(c_k[:, h], q_t[h]) * SCORE_SCALE)
        weight = prob.astype(BF)
        d_score = score_grad(prob, mm(c_v[:, h], a_t[h]))
        out_t.append(mm(c_vt[i * 16 : (i + 1) * 16], weight))
        gq_t.append(mm(c_kt[h], d_score))
        gck_t.append(mm_nt(q_t[h], d_score))
        gcv_t.append(mm_nt(a_t[h], weight))
    gck_t = jnp.concatenate(gck_t, 0).astype(BF)
    gcv_t = jnp.concatenate(gcv_t, 0).astype(BF)

    grad_state_t = mm(jnp.concatenate([wk, wv], 1), jnp.concatenate([gck_t, gcv_t], 0))
    gs_t = grad_state_t.astype(BF)
    gsq_t = []
    gsk_t = []
    gsv_t = []
    for h, prob, weight in zip(heads, s_prob, s_weight):
        d_score = score_grad(prob, mm(s_v[:, h], gs_t[h]))
        gsq_t.append(mm(s_kt[h], d_score))
        gsk_t.append(mm_nt(s_qt[h], d_score))
        gsv_t.append(mm_nt(gs_t[h], weight))
    gsq_t = jnp.concatenate(gsq_t, 0).astype(BF)
    gsk_t = jnp.concatenate(gsk_t, 0).astype(BF)
    gsv_t = jnp.concatenate(gsv_t, 0).astype(BF)
    grad_pooled_t = grad_state_t + mm(
        jnp.concatenate([wq, wk, wv], 1), jnp.concatenate([gsq_t, gsk_t, gsv_t], 0)
    )
    share = grad_pooled_t.T * inverse

    near_gq = jnp.concatenate([near_gq_ref[...], section(4).astype(F32)], 1)
    gq_t = (near_gq + jnp.concatenate(gq_t, 0)).astype(BF)
    gq_t_ref[...] = gq_t[:, :NODES]
    near_t = jnp.concatenate([near_t_ref[...], section(3).astype(F32)], 1)
    attended_t = (near_t + jnp.concatenate(out_t, 0)).astype(BF)
    x_t = jnp.concatenate([xt_ref[...], section(2)], 1)
    grad_out = jnp.concatenate([grad_ref[...], folded(5)], 0)
    near_kv = section(6).astype(F32)
    rows = near_kv.shape[0] // 4
    near_k = wkv_ref[0] + jnp.concatenate([near_kv[:rows], near_kv[rows : 2 * rows]], 1)
    near_v = wkv_ref[1] + jnp.concatenate([near_kv[2 * rows : 3 * rows], near_kv[3 * rows :]], 1)
    grads = [
        mm_nt(jnp.concatenate([x_t, low_rank[:, :SUP]], 1), jnp.concatenate([gq_t, gsq_t], 1)),
        near_k + mm_nt(low_rank, jnp.concatenate([gsk_t, gck_t], 1)),
        near_v + mm_nt(low_rank, jnp.concatenate([gsv_t, gcv_t], 1)),
        mm(attended_t, grad_out),
    ]
    half = SUP // 2
    first = jnp.broadcast_to(core, (half, WIDTH)) == 0
    pooled_half = jnp.where(first, share[:half], share[half:])
    quarter = half // len(grads)
    message_rows = message_ref.shape[1]
    n_z = message_ref.shape[0] // len(grads)
    own_rows = message_rows - quarter
    for w, grad in enumerate(grads):
        piece = pooled_half[w * quarter : (w + 1) * quarter]
        for z in range(n_z):
            rows = grad[z * own_rows : (z + 1) * own_rows]
            message_ref[w * n_z + z] = jnp.concatenate([rows, piece], 0).astype(BF)


def back_body(grad_kv_ref, grad_ref, wk_ref, wv_ref, base_ref, below_ref, above_ref):
    grad_kv = flip(grad_kv_ref[...])
    back = mm_nt(grad_kv[:, :WIDTH], wk_ref[...]) + mm_nt(grad_kv[:, WIDTH:], wv_ref[...])
    base_ref[...] = grad_ref[...].astype(F32) + back[HALO : HALO + NODES]
    below_ref[...] = back[:HALO].astype(BF)
    above_ref[...] = back[HALO + NODES :].astype(BF)


def own_body(base_ref, gq_t_ref, wq_ref, below_ref, above_ref, out_ref):
    own = base_ref[...] + mm_nt(flip(gq_t_ref[...]), wq_ref[...])
    out_ref[:HALO] = own[:HALO] + below_ref[...].astype(F32)
    out_ref[HALO : NODES - HALO] = own[HALO : NODES - HALO]
    out_ref[NODES - HALO :] = own[NODES - HALO :] + above_ref[...].astype(F32)


def shares_body(n_w, pieces_ref, own_ref, out_ref, pooled_ref):
    n_z = pieces_ref.shape[0] // n_w
    sums = [jnp.sum(pieces_ref[w * n_z : (w + 1) * n_z].astype(F32), 0) for w in range(n_w)]
    rows = out_ref.shape[1]
    share = sum(part[:rows] for part in sums).astype(BF)
    for y in range(out_ref.shape[0]):
        out_ref[y] = share
    pooled_ref[...] = jnp.concatenate([part[rows:] for part in sums], 0).astype(BF)


def columns_body(parts_ref, pooled_ref, out_ref):
    share = jnp.sum(parts_ref[...].astype(F32), 0)
    pooled = pooled_ref[...].astype(F32)
    n_w = out_ref.shape[0]
    quarter = pooled.shape[1] // n_w
    for w in range(n_w):
        rows = slice(w * quarter, (w + 1) * quarter)
        out_ref[w] = jnp.concatenate([share, pooled[0, rows], pooled[1, rows]], 0).astype(BF)


def final_body(scale, parts_ref, own_ref, cluster_ref, weights_ref, nodes_ref):
    n_w, rows, _ = weights_ref.shape
    quarter = (parts_ref.shape[1] - rows) // 2
    parts = parts_ref[...].astype(F32)
    weights_ref[...] = parts[:, :rows] * scale
    halves = [parts[w, rows + c * quarter : rows + (c + 1) * quarter] for c in range(2) for w in range(n_w)]
    pooled = jnp.concatenate(halves, 0).astype(BF)
    member = (cluster_ref[...] == iota((SUP, NODES), 0)).astype(F32).T.astype(BF)
    nodes_ref[...] = (own_ref[...] + mm(member, pooled)).astype(BF)


def swap(parts, axes):
    return lax.all_to_all(parts, axes, 0, 0, tiled=True)


def local(sizes, node_feats, grad_out, neighbours, cluster, super_links, w_query, w_key, w_value, w_out):
    n_x, n_y, n_z, n_c = sizes
    n_super = n_z * n_c
    n_dom = n_x * n_y
    supers = ("z", "c")
    up = [(i, (i + 1) % n_super) for i in range(n_super)]
    down = [(i, (i + n_super - 1) % n_super) for i in range(n_super)]
    cluster_row = cluster.reshape(1, NODES)
    sums, first_rows, last_rows, allowed = call(
        sums_body,
        "cluster_sums",
        [((n_z, SUM_ROWS, WIDTH), BF), ((HALO, WIDTH), BF), ((HALO, WIDTH), BF), ((SUP, SUP), F32)],
        [
            ((NODES, WIDTH), BF), ((1, NODES), jnp.int32), ((K_TOP, SUP), jnp.int32),
            pltpu.SemaphoreType.DMA((3,)),
        ],
        1 << 22,
        node_feats, cluster_row, super_links.T,
        outside=(0, 1, 2),
        vmem=60,
    )
    core = lax.axis_index("c").reshape(1)
    low = lax.ppermute(last_rows, supers, up)
    high = lax.ppermute(first_rows, supers, down)
    order = [[z // 2 if z % 2 == 0 else n_z - 1 - z // 2 for z in range(n_z)]]
    parts = lax.all_to_all(sums, "z", 0, 0, axis_index_groups=order, tiled=True)
    parts = lax.all_gather(parts, "c", tiled=True)
    q_t, a_t, x_t, w_t, near_t, near_gq, wkv, grad_kv, chip = call(
        near_body,
        "near_attention",
        [
            ((WIDTH, NODES), BF), ((WIDTH, NODES), BF), ((WIDTH // 2, NODES), BF), ((3 * WIDTH, WIDTH), BF),
            ((WIDTH // 2, NODES), F32), ((WIDTH, NODES), F32), ((2, WIDTH // 2, WIDTH), F32), ((2 * WIDTH, EXT), BF),
            ((CHIP_AT[-1], NODES), BF),
        ],
        [
            ((WIDTH, NODES), F32),
        ],
        10 << 30,
        low, node_feats, high, grad_out, neighbours.T, core, w_query, w_key, w_value, w_out,
    )
    base, below, above = call(
        back_body,
        "halo_returns",
        [((NODES, WIDTH), F32), ((HALO, WIDTH), BF), ((HALO, WIDTH), BF)],
        [],
        1 << 28,
        grad_kv, grad_out, w_key, w_value,
    )
    from_above = lax.ppermute(below, supers, down)
    from_below = lax.ppermute(above, supers, up)
    share_rows = WIDTH // n_super
    half = (SUP // 2, WIDTH)
    message_rows = share_rows + SUP // 2 // n_x
    pieces, gq_t = call(
        far_body,
        "far_attention",
        [((n_x * n_z, message_rows, WIDTH), BF), ((WIDTH, NODES), BF)],
        [],
        10 << 30,
        parts, allowed, lax.all_gather(chip, "c"), grad_out, w_query, w_key, w_value, w_t,
        q_t, a_t, x_t, near_t, near_gq, wkv, core,
    )
    pieces = swap(pieces, ("x", "z"))
    (own,) = call(
        own_body, "own_nodes", [((NODES, WIDTH), F32)], [], 1 << 28, base, gq_t, w_query, from_below, from_above
    )
    shares, pooled = call(
        functools.partial(shares_body, n_x),
        "weight_shares",
        [((n_y, share_rows, WIDTH), BF), (half, BF)],
        [],
        1 << 20,
        pieces, own,
        outside=(1,),
    )
    shares = swap(shares, "y")
    (columns,) = call(
        columns_body,
        "weight_columns",
        [((n_x, message_rows + SUP // 2 // n_x, WIDTH), BF)],
        [],
        1 << 20,
        shares, lax.all_gather(pooled, "c"),
    )
    columns = swap(columns, "x")
    scale = 1.0 / math.sqrt(NODES * n_super * n_dom)
    grad_weights, grad_nodes = call(
        functools.partial(final_body, scale),
        "gradients",
        [((4, share_rows, WIDTH), F32), ((NODES, WIDTH), BF)],
        [],
        1 << 20,
        columns, own, cluster_row,
    )
    return grad_nodes, grad_weights


def solution(mesh):
    n_dom = mesh.shape["dom"]
    n_super = mesh.shape["super"]
    sizes = (4, n_dom // 4, n_super // 2, 2)
    fine = Mesh(mesh.devices.reshape(sizes), ("x", "y", "z", "c"))
    everyone = ("x", "y", "z", "c")
    return jax.shard_map(
        functools.partial(local, sizes),
        mesh=fine,
        in_specs=(
            P(everyone, None),
            P(everyone, None),
            P(everyone, None),
            P(everyone),
            P(("x", "y"), None),
            P(),
            P(),
            P(),
            P(),
        ),
        out_specs=(P(everyone, None), P(None, ("z", "c"), None)),
        check_vma=False,
    )
```

```python
import functools
import math

import jax
import jax.numpy as jnp
from jax import lax
from jax.experimental import pallas as pl
from jax.experimental.pallas import tpu as pltpu
from jax.sharding import Mesh, PartitionSpec as P

WIDTH = 256
HEADS = 8
HEAD_DIM = 32
NODES = 128
HALO = 32
EXT = NODES + 2 * HALO
SUP = 64
K_TOP = 8
SUM_ROWS = SUP + 8
CHIP_ROWS = (256, 256, 128, 128, 256, 256, 512)
CHIP_AT = tuple(sum(CHIP_ROWS[:i]) for i in range(len(CHIP_ROWS) + 1))
SCORE_SCALE = 1.0 / math.sqrt(HEAD_DIM)
NEVER = -1e30
BF = jnp.bfloat16
F32 = jnp.float32


def mm(a, b):
    return jnp.dot(a, b, preferred_element_type=F32)


def mm_nt(a, b):
    return lax.dot_general(a, b, (((1,), (1,)), ((), ())), preferred_element_type=F32)


def iota(shape, dim):
    return lax.broadcasted_iota(jnp.int32, shape, dim)


def flip(a):
    return a.astype(F32).T.astype(a.dtype)


def rows_of(h):
    return slice(h * HEAD_DIM, (h + 1) * HEAD_DIM)


def split_rows(m, core):
    pairs = m.reshape(m.shape[0] // 32, 2, 16, m.shape[1])
    low, high = pairs[:, 0], pairs[:, 1]
    first = jnp.broadcast_to(core, low.shape) == 0
    shape = (m.shape[0] // 2, m.shape[1])
    return jnp.where(first, low, high).reshape(shape), jnp.where(first, high, low).reshape(shape)


def call(body, name, outs, scratch, flops, *args, outside=(), vmem=32):
    size = sum(a.size * a.dtype.itemsize for a in args)
    inside = pl.BlockSpec(memory_space=pltpu.VMEM)
    smem = pl.BlockSpec(memory_space=pltpu.SMEM)
    anywhere = pl.BlockSpec(memory_space=pltpu.HBM)
    return pl.pallas_call(
        body,
        in_specs=[anywhere if i in outside else smem if a.ndim == 1 else inside for i, a in enumerate(args)],
        name=name,
        out_shape=tuple(jax.ShapeDtypeStruct(s, d) for s, d in outs),
        scratch_shapes=[pltpu.VMEM(*s) if isinstance(s, tuple) else s for s in scratch],
        compiler_params=pltpu.CompilerParams(vmem_limit_bytes=vmem * 1024 * 1024),
        cost_estimate=pl.CostEstimate(flops=flops, bytes_accessed=size, transcendentals=0),
    )(*args)


def softmax_rows(scores):
    e = jnp.exp(scores)
    return e / jnp.sum(e, 0, keepdims=True)


def score_grad(prob, g):
    return (prob * (g - jnp.sum(prob * g, 0, keepdims=True)) * SCORE_SCALE).astype(BF)


def sums_body(
    x_any, cluster_any, links_any, out_ref, low_ref, high_ref, allowed_ref, x_ref, cluster_ref, links_ref, sems
):
    copies = [
        pltpu.make_async_copy(cluster_any, cluster_ref, sems.at[0]),
        pltpu.make_async_copy(x_any, x_ref, sems.at[1]),
        pltpu.make_async_copy(links_any, links_ref, sems.at[2]),
    ]
    for copy in copies:
        copy.start()
    for copy in copies:
        copy.wait()
    member = (cluster_ref[...] == iota((SUP, NODES), 0)).astype(F32)
    sums = mm(member.astype(BF), x_ref[...])
    counts = jnp.sum(member, 1, keepdims=True)
    diagonal = iota((SUP, WIDTH), 0) == iota((SUP, WIDTH), 1)
    count_row = jnp.sum(jnp.where(diagonal, counts, 0.0), 0, keepdims=True)
    count_rows = jnp.broadcast_to(count_row, (SUM_ROWS - SUP, WIDTH))
    message = jnp.concatenate([sums, count_rows], 0).astype(BF)
    for peer in range(out_ref.shape[0]):
        out_ref[peer] = message
    low_ref[...] = x_ref[:HALO]
    high_ref[...] = x_ref[NODES - HALO :]
    links = links_ref[...]
    target = iota((SUP, SUP), 0)
    linked = links[:1] == target
    for l in range(1, links.shape[0]):
        linked = jnp.logical_or(linked, links[l : l + 1] == target)
    allowed_ref[...] = jnp.where(linked, 0.0, NEVER)


def near_body(
    low_ref, x_ref, high_ref, grad_ref, slots_ref, core_ref, wq_ref, wk_ref, wv_ref, wo_ref,
    qt_ref, at_ref, xt_ref, wt_ref, out_t_ref, gq_t_ref, wkv_ref, grad_kv_ref, chip_ref,
    near_t,
):
    ext = jnp.concatenate([low_ref[...], x_ref[...], high_ref[...]], 0)
    wk = wk_ref[...]
    wv = wv_ref[...]
    queries = mm(x_ref[...], wq_ref[...]).astype(BF)
    keys = mm(ext, wk).astype(BF)
    vals = mm(ext, wv).astype(BF)
    grad_attn = mm_nt(grad_ref[...], wo_ref[...]).astype(BF)
    q_t = flip(queries)
    a_t = flip(grad_attn)
    keys_t = flip(keys)
    vals_t = flip(vals)
    qt_ref[...] = q_t
    at_ref[...] = a_t
    slots = slots_ref[...]
    row = iota((EXT, NODES), 0)
    count = jnp.zeros((EXT, NODES), F32)
    for j in range(slots.shape[0]):
        count = count + jnp.where(slots[j : j + 1] == row, 1.0, 0.0)
    log_count = jnp.where(count > 0.0, jnp.log(jnp.maximum(count, 1.0)), NEVER)
    gk_t = []
    gv_t = []
    for h in range(HEADS):
        rows = rows_of(h)
        prob = softmax_rows(mm(keys[:, rows], q_t[rows]) * SCORE_SCALE + log_count)
        weight = prob.astype(BF)
        d_score = score_grad(prob, mm(vals[:, rows], a_t[rows]))
        near_t[rows] = mm(vals_t[rows], weight)
        gq_t_ref[rows] = mm(keys_t[rows], d_score)
        gk_t.append(mm_nt(q_t[rows], d_score))
        gv_t.append(mm_nt(a_t[rows], weight))
    gk_t = jnp.concatenate(gk_t, 0).astype(BF)
    gv_t = jnp.concatenate(gv_t, 0).astype(BF)
    grad_kv_ref[:WIDTH] = gk_t
    grad_kv_ref[WIDTH:] = gv_t
    core = core_ref[0]
    ext_t = ext.astype(F32).T
    wt_ref[:WIDTH] = flip(wq_ref[...])
    wt_ref[WIDTH : 2 * WIDTH] = flip(wk)
    wt_ref[2 * WIDTH :] = flip(wv)
    x_mine, x_other = split_rows(ext_t[:, HALO : HALO + NODES], core)
    xt_ref[...] = x_mine.astype(BF)
    near_mine, near_other = split_rows(near_t[...], core)
    out_t_ref[...] = near_mine
    ext_t = ext_t.astype(BF)
    key_mine, key_other = split_rows(mm_nt(ext_t, gk_t), core)
    val_mine, val_other = split_rows(mm_nt(ext_t, gv_t), core)
    wkv_ref[0] = key_mine
    wkv_ref[1] = val_mine
    chip = [
        q_t, a_t, x_other, near_other, gq_t_ref[...], grad_ref[:, :NODES], grad_ref[:, NODES:],
        key_other[:, :NODES], key_other[:, NODES:], val_other[:, :NODES], val_other[:, NODES:],
    ]
    at = 0
    for part in chip:
        chip_ref[at : at + part.shape[0]] = part.astype(BF)
        at += part.shape[0]


def far_body(
    parts_ref, allowed_ref, both_ref, grad_ref, wq_ref, wk_ref, wv_ref, wt_ref,
    qt_ref, at_ref, xt_ref, near_t_ref, near_gq_ref, wkv_ref, core_ref,
    message_ref, gq_t_ref,
):
    core = core_ref[0]
    sibling = both_ref.at[1 - core]

    def section(i):
        return sibling[CHIP_AT[i] : CHIP_AT[i + 1]]

    def folded(i):
        rows = section(i)
        half = rows.shape[0] // 2
        return jnp.concatenate([rows[:half], rows[half:]], 1)

    heads = [rows_of(h) for h in range(HEADS)]
    wq = wq_ref[...]
    wk = wk_ref[...]
    wv = wv_ref[...]
    wt = wt_ref[...]
    totals = jnp.sum(parts_ref[...].astype(F32), 0)
    diagonal = iota((SUP, WIDTH), 0) == iota((SUP, WIDTH), 1)
    counts = jnp.sum(jnp.where(diagonal, totals[SUP : SUP + 1], 0.0), 1, keepdims=True)
    inverse = 1.0 / jnp.maximum(counts, 1.0)
    pooled = (totals[:SUP] * inverse).astype(BF)
    pooled_t = flip(pooled)

    s_proj_t = mm(wt, pooled_t).astype(BF)
    s_qt, s_kt, s_vt = (s_proj_t[i * WIDTH : (i + 1) * WIDTH] for i in range(3))
    s_k = mm(pooled, wk).astype(BF)
    s_v = mm(pooled, wv).astype(BF)
    allowed = allowed_ref[...]
    s_prob = [softmax_rows(mm(s_k[:, h], s_qt[h]) * SCORE_SCALE + allowed) for h in heads]
    s_weight = [p.astype(BF) for p in s_prob]
    moved_t = jnp.concatenate([mm(s_vt[h], w) for h, w in zip(heads, s_weight)], 0)
    state_t = pooled_t.astype(F32) + moved_t
    low_rank = jnp.concatenate(
        [split_rows(pooled_t.astype(F32), core)[0], split_rows(state_t, core)[0]], 1
    ).astype(BF)
    state_t = state_t.astype(BF)
    state = flip(state_t)

    c_proj_t = mm(wt[WIDTH:], state_t)
    c_kt = c_proj_t[:WIDTH].astype(BF)
    c_vt = split_rows(c_proj_t[WIDTH:], core)[0].astype(BF)
    c_k = mm(state, wk).astype(BF)
    c_v = mm(state, wv).astype(BF)
    q_t = jnp.concatenate([qt_ref[...], section(0)], 1)
    a_t = jnp.concatenate([at_ref[...], section(1)], 1)
    out_t = []
    gq_t = []
    gck_t = []
    gcv_t = []
    for i, h in enumerate(heads):
        prob = softmax_rows(mm(c_k[:, h], q_t[h]) * SCORE_SCALE)
        weight = prob.astype(BF)
        d_score = score_grad(prob, mm(c_v[:, h], a_t[h]))
        out_t.append(mm(c_vt[i * 16 : (i + 1) * 16], weight))
        gq_t.append(mm(c_kt[h], d_score))
        gck_t.append(mm_nt(q_t[h], d_score))
        gcv_t.append(mm_nt(a_t[h], weight))
    gck_t = jnp.concatenate(gck_t, 0).astype(BF)
    gcv_t = jnp.concatenate(gcv_t, 0).astype(BF)

    grad_state_t = mm(jnp.concatenate([wk, wv], 1), jnp.concatenate([gck_t, gcv_t], 0))
    gs_t = grad_state_t.astype(BF)
    gsq_t = []
    gsk_t = []
    gsv_t = []
    for h, prob, weight in zip(heads, s_prob, s_weight):
        d_score = score_grad(prob, mm(s_v[:, h], gs_t[h]))
        gsq_t.append(mm(s_kt[h], d_score))
        gsk_t.append(mm_nt(s_qt[h], d_score))
        gsv_t.append(mm_nt(gs_t[h], weight))
    gsq_t = jnp.concatenate(gsq_t, 0).astype(BF)
    gsk_t = jnp.concatenate(gsk_t, 0).astype(BF)
    gsv_t = jnp.concatenate(gsv_t, 0).astype(BF)
    grad_pooled_t = grad_state_t + mm(
        jnp.concatenate([wq, wk, wv], 1), jnp.concatenate([gsq_t, gsk_t, gsv_t], 0)
    )
    share = grad_pooled_t.T * inverse

    near_gq = jnp.concatenate([near_gq_ref[...], section(4).astype(F32)], 1)
    gq_t = (near_gq + jnp.concatenate(gq_t, 0)).astype(BF)
    gq_t_ref[...] = gq_t[:, :NODES]
    near_t = jnp.concatenate([near_t_ref[...], section(3).astype(F32)], 1)
    attended_t = (near_t + jnp.concatenate(out_t, 0)).astype(BF)
    x_t = jnp.concatenate([xt_ref[...], section(2)], 1)
    grad_out = jnp.concatenate([grad_ref[...], folded(5)], 0)
    near_kv = section(6).astype(F32)
    rows = near_kv.shape[0] // 4
    near_k = wkv_ref[0] + jnp.concatenate([near_kv[:rows], near_kv[rows : 2 * rows]], 1)
    near_v = wkv_ref[1] + jnp.concatenate([near_kv[2 * rows : 3 * rows], near_kv[3 * rows :]], 1)
    grads = [
        mm_nt(jnp.concatenate([x_t, low_rank[:, :SUP]], 1), jnp.concatenate([gq_t, gsq_t], 1)),
        near_k + mm_nt(low_rank, jnp.concatenate([gsk_t, gck_t], 1)),
        near_v + mm_nt(low_rank, jnp.concatenate([gsv_t, gcv_t], 1)),
        mm(attended_t, grad_out),
    ]
    half = SUP // 2
    first = jnp.broadcast_to(core, (half, WIDTH)) == 0
    pooled_half = jnp.where(first, share[:half], share[half:])
    quarter = half // len(grads)
    message_rows = message_ref.shape[1]
    n_z = message_ref.shape[0] // len(grads)
    own_rows = message_rows - quarter
    for w, grad in enumerate(grads):
        piece = pooled_half[w * quarter : (w + 1) * quarter]
        for z in range(n_z):
            rows = grad[z * own_rows : (z + 1) * own_rows]
            message_ref[w * n_z + z] = jnp.concatenate([rows, piece], 0).astype(BF)


def back_body(grad_kv_ref, grad_ref, wk_ref, wv_ref, base_ref, below_ref, above_ref):
    grad_kv = flip(grad_kv_ref[...])
    back = mm_nt(grad_kv[:, :WIDTH], wk_ref[...]) + mm_nt(grad_kv[:, WIDTH:], wv_ref[...])
    base_ref[...] = grad_ref[...].astype(F32) + back[HALO : HALO + NODES]
    below_ref[...] = back[:HALO].astype(BF)
    above_ref[...] = back[HALO + NODES :].astype(BF)


def own_body(base_ref, gq_t_ref, wq_ref, below_ref, above_ref, out_ref):
    own = base_ref[...] + mm_nt(flip(gq_t_ref[...]), wq_ref[...])
    out_ref[:HALO] = own[:HALO] + below_ref[...].astype(F32)
    out_ref[HALO : NODES - HALO] = own[HALO : NODES - HALO]
    out_ref[NODES - HALO :] = own[NODES - HALO :] + above_ref[...].astype(F32)


def shares_body(n_w, pieces_ref, own_ref, out_ref, pooled_ref):
    n_z = pieces_ref.shape[0] // n_w
    sums = [jnp.sum(pieces_ref[w * n_z : (w + 1) * n_z].astype(F32), 0) for w in range(n_w)]
    rows = out_ref.shape[1]
    share = sum(part[:rows] for part in sums).astype(BF)
    for y in range(out_ref.shape[0]):
        out_ref[y] = share
    pooled_ref[...] = jnp.concatenate([part[rows:] for part in sums], 0).astype(BF)


def columns_body(parts_ref, pooled_ref, out_ref):
    share = jnp.sum(parts_ref[...].astype(F32), 0)
    pooled = pooled_ref[...].astype(F32)
    n_w = out_ref.shape[0]
    quarter = pooled.shape[1] // n_w
    for w in range(n_w):
        rows = slice(w * quarter, (w + 1) * quarter)
        out_ref[w] = jnp.concatenate([share, pooled[0, rows], pooled[1, rows]], 0).astype(BF)


def final_body(scale, parts_ref, own_ref, cluster_ref, weights_ref, nodes_ref):
    n_w, rows, _ = weights_ref.shape
    quarter = (parts_ref.shape[1] - rows) // 2
    parts = parts_ref[...].astype(F32)
    weights_ref[...] = parts[:, :rows] * scale
    halves = [parts[w, rows + c * quarter : rows + (c + 1) * quarter] for c in range(2) for w in range(n_w)]
    pooled = jnp.concatenate(halves, 0).astype(BF)
    member = (cluster_ref[...] == iota((SUP, NODES), 0)).astype(F32).T.astype(BF)
    nodes_ref[...] = (own_ref[...] + mm(member, pooled)).astype(BF)


def swap(parts, axes):
    return lax.all_to_all(parts, axes, 0, 0, tiled=True)


def local(sizes, node_feats, grad_out, neighbours, cluster, super_links, w_query, w_key, w_value, w_out):
    n_x, n_y, n_z, n_c = sizes
    n_super = n_z * n_c
    n_dom = n_x * n_y
    supers = ("z", "c")
    up = [(i, (i + 1) % n_super) for i in range(n_super)]
    down = [(i, (i + n_super - 1) % n_super) for i in range(n_super)]
    cluster_row = cluster.reshape(1, NODES)
    sums, first_rows, last_rows, allowed = call(
        sums_body,
        "cluster_sums",
        [((n_z, SUM_ROWS, WIDTH), BF), ((HALO, WIDTH), BF), ((HALO, WIDTH), BF), ((SUP, SUP), F32)],
        [
            ((NODES, WIDTH), BF), ((1, NODES), jnp.int32), ((K_TOP, SUP), jnp.int32),
            pltpu.SemaphoreType.DMA((3,)),
        ],
        1 << 22,
        node_feats, cluster_row, super_links.T,
        outside=(0, 1, 2),
        vmem=60,
    )
    core = lax.axis_index("c").reshape(1)
    low = lax.ppermute(last_rows, supers, up)
    high = lax.ppermute(first_rows, supers, down)
    order = [[z // 2 if z % 2 == 0 else n_z - 1 - z // 2 for z in range(n_z)]]
    parts = lax.all_to_all(sums, "z", 0, 0, axis_index_groups=order, tiled=True)
    parts = lax.all_gather(parts, "c", tiled=True)
    q_t, a_t, x_t, w_t, near_t, near_gq, wkv, grad_kv, chip = call(
        near_body,
        "near_attention",
        [
            ((WIDTH, NODES), BF), ((WIDTH, NODES), BF), ((WIDTH // 2, NODES), BF), ((3 * WIDTH, WIDTH), BF),
            ((WIDTH // 2, NODES), F32), ((WIDTH, NODES), F32), ((2, WIDTH // 2, WIDTH), F32), ((2 * WIDTH, EXT), BF),
            ((CHIP_AT[-1], NODES), BF),
        ],
        [
            ((WIDTH, NODES), F32),
        ],
        10 << 30,
        low, node_feats, high, grad_out, neighbours.T, core, w_query, w_key, w_value, w_out,
    )
    base, below, above = call(
        back_body,
        "halo_returns",
        [((NODES, WIDTH), F32), ((HALO, WIDTH), BF), ((HALO, WIDTH), BF)],
        [],
        1 << 28,
        grad_kv, grad_out, w_key, w_value,
    )
    from_above = lax.ppermute(below, supers, down)
    from_below = lax.ppermute(above, supers, up)
    share_rows = WIDTH // n_super
    half = (SUP // 2, WIDTH)
    message_rows = share_rows + SUP // 2 // n_x
    pieces, gq_t = call(
        far_body,
        "far_attention",
        [((n_x * n_z, message_rows, WIDTH), BF), ((WIDTH, NODES), BF)],
        [],
        10 << 30,
        parts, allowed, lax.all_gather(chip, "c"), grad_out, w_query, w_key, w_value, w_t,
        q_t, a_t, x_t, near_t, near_gq, wkv, core,
    )
    pieces = swap(pieces, ("x", "z"))
    (own,) = call(
        own_body, "own_nodes", [((NODES, WIDTH), F32)], [], 1 << 28, base, gq_t, w_query, from_below, from_above
    )
    shares, pooled = call(
        functools.partial(shares_body, n_x),
        "weight_shares",
        [((n_y, share_rows, WIDTH), BF), (half, BF)],
        [],
        1 << 20,
        pieces, own,
        outside=(1,),
    )
    shares = swap(shares, "y")
    (columns,) = call(
        columns_body,
        "weight_columns",
        [((n_x, message_rows + SUP // 2 // n_x, WIDTH), BF)],
        [],
        1 << 20,
        shares, lax.all_gather(pooled, "c"),
    )
    columns = swap(columns, "x")
    scale = 1.0 / math.sqrt(NODES * n_super * n_dom)
    grad_weights, grad_nodes = call(
        functools.partial(final_body, scale),
        "gradients",
        [((4, share_rows, WIDTH), F32), ((NODES, WIDTH), BF)],
        [],
        1 << 20,
        columns, own, cluster_row,
    )
    return grad_nodes, grad_weights


def solution(mesh):
    n_dom = mesh.shape["dom"]
    n_super = mesh.shape["super"]
    sizes = (4, n_dom // 4, n_super // 2, 2)
    fine = Mesh(mesh.devices.reshape(sizes), ("x", "y", "z", "c"))
    everyone = ("x", "y", "z", "c")
    return jax.shard_map(
        functools.partial(local, sizes),
        mesh=fine,
        in_specs=(
            P(everyone, None),
            P(everyone, None),
            P(everyone, None),
            P(everyone),
            P(("x", "y"), None),
            P(),
            P(),
            P(),
            P(),
        ),
        out_specs=(P(everyone, None), P(None, ("z", "c"), None)),
        check_vma=False,
    )
```

```python
import functools
import math

import jax
import jax.numpy as jnp
from jax import lax
from jax.experimental import pallas as pl
from jax.experimental.pallas import tpu as pltpu
from jax.sharding import Mesh, PartitionSpec as P

WIDTH = 256
HEADS = 8
HEAD_DIM = 32
NODES = 128
HALO = 32
EXT = NODES + 2 * HALO
SUP = 64
K_TOP = 8
SUM_ROWS = SUP + 8
CHIP_ROWS = (256, 256, 128, 128, 256, 256, 512)
CHIP_AT = tuple(sum(CHIP_ROWS[:i]) for i in range(len(CHIP_ROWS) + 1))
SCORE_SCALE = 1.0 / math.sqrt(HEAD_DIM)
NEVER = -1e30
BF = jnp.bfloat16
F32 = jnp.float32


def mm(a, b):
    return jnp.dot(a, b, preferred_element_type=F32)


def mm_nt(a, b):
    return lax.dot_general(a, b, (((1,), (1,)), ((), ())), preferred_element_type=F32)


def iota(shape, dim):
    return lax.broadcasted_iota(jnp.int32, shape, dim)


def flip(a):
    return a.astype(F32).T.astype(a.dtype)


def rows_of(h):
    return slice(h * HEAD_DIM, (h + 1) * HEAD_DIM)


def split_rows(m, core):
    pairs = m.reshape(m.shape[0] // 32, 2, 16, m.shape[1])
    low, high = pairs[:, 0], pairs[:, 1]
    first = jnp.broadcast_to(core, low.shape) == 0
    shape = (m.shape[0] // 2, m.shape[1])
    return jnp.where(first, low, high).reshape(shape), jnp.where(first, high, low).reshape(shape)


def call(body, name, outs, scratch, flops, *args, outside=(), vmem=32):
    size = sum(a.size * a.dtype.itemsize for a in args)
    inside = pl.BlockSpec(memory_space=pltpu.VMEM)
    smem = pl.BlockSpec(memory_space=pltpu.SMEM)
    anywhere = pl.BlockSpec(memory_space=pltpu.HBM)
    return pl.pallas_call(
        body,
        in_specs=[anywhere if i in outside else smem if a.ndim == 1 else inside for i, a in enumerate(args)],
        name=name,
        out_shape=tuple(jax.ShapeDtypeStruct(s, d) for s, d in outs),
        scratch_shapes=[pltpu.VMEM(*s) if isinstance(s, tuple) else s for s in scratch],
        compiler_params=pltpu.CompilerParams(vmem_limit_bytes=vmem * 1024 * 1024),
        cost_estimate=pl.CostEstimate(flops=flops, bytes_accessed=size, transcendentals=0),
    )(*args)


def softmax_rows(scores):
    e = jnp.exp(scores)
    return e / jnp.sum(e, 0, keepdims=True)


def score_grad(prob, g):
    return (prob * (g - jnp.sum(prob * g, 0, keepdims=True)) * SCORE_SCALE).astype(BF)


def sums_body(
    x_any, cluster_any, links_any, out_ref, low_ref, high_ref, allowed_ref, x_ref, cluster_ref, links_ref, sems
):
    copies = [
        pltpu.make_async_copy(cluster_any, cluster_ref, sems.at[0]),
        pltpu.make_async_copy(x_any, x_ref, sems.at[1]),
        pltpu.make_async_copy(links_any, links_ref, sems.at[2]),
    ]
    for copy in copies:
        copy.start()
    for copy in copies:
        copy.wait()
    member = (cluster_ref[...] == iota((SUP, NODES), 0)).astype(F32)
    sums = mm(member.astype(BF), x_ref[...])
    counts = jnp.sum(member, 1, keepdims=True)
    diagonal = iota((SUP, WIDTH), 0) == iota((SUP, WIDTH), 1)
    count_row = jnp.sum(jnp.where(diagonal, counts, 0.0), 0, keepdims=True)
    count_rows = jnp.broadcast_to(count_row, (SUM_ROWS - SUP, WIDTH))
    message = jnp.concatenate([sums, count_rows], 0).astype(BF)
    for peer in range(out_ref.shape[0]):
        out_ref[peer] = message
    low_ref[...] = x_ref[:HALO]
    high_ref[...] = x_ref[NODES - HALO :]
    links = links_ref[...]
    target = iota((SUP, SUP), 0)
    linked = links[:1] == target
    for l in range(1, links.shape[0]):
        linked = jnp.logical_or(linked, links[l : l + 1] == target)
    allowed_ref[...] = jnp.where(linked, 0.0, NEVER)


def near_body(
    low_ref, x_ref, high_ref, grad_ref, slots_ref, core_ref, wq_ref, wk_ref, wv_ref, wo_ref,
    qt_ref, at_ref, xt_ref, wt_ref, out_t_ref, gq_t_ref, wkv_ref, grad_kv_ref, chip_ref,
    near_t,
):
    ext = jnp.concatenate([low_ref[...], x_ref[...], high_ref[...]], 0)
    wk = wk_ref[...]
    wv = wv_ref[...]
    queries = mm(x_ref[...], wq_ref[...]).astype(BF)
    keys = mm(ext, wk).astype(BF)
    vals = mm(ext, wv).astype(BF)
    grad_attn = mm_nt(grad_ref[...], wo_ref[...]).astype(BF)
    q_t = flip(queries)
    a_t = flip(grad_attn)
    keys_t = flip(keys)
    vals_t = flip(vals)
    qt_ref[...] = q_t
    at_ref[...] = a_t
    slots = slots_ref[...]
    row = iota((EXT, NODES), 0)
    count = jnp.zeros((EXT, NODES), F32)
    for j in range(slots.shape[0]):
        count = count + jnp.where(slots[j : j + 1] == row, 1.0, 0.0)
    log_count = jnp.where(count > 0.0, jnp.log(jnp.maximum(count, 1.0)), NEVER)
    gk_t = []
    gv_t = []
    for h in range(HEADS):
        rows = rows_of(h)
        prob = softmax_rows(mm(keys[:, rows], q_t[rows]) * SCORE_SCALE + log_count)
        weight = prob.astype(BF)
        d_score = score_grad(prob, mm(vals[:, rows], a_t[rows]))
        near_t[rows] = mm(vals_t[rows], weight)
        gq_t_ref[rows] = mm(keys_t[rows], d_score)
        gk_t.append(mm_nt(q_t[rows], d_score))
        gv_t.append(mm_nt(a_t[rows], weight))
    gk_t = jnp.concatenate(gk_t, 0).astype(BF)
    gv_t = jnp.concatenate(gv_t, 0).astype(BF)
    grad_kv_ref[:WIDTH] = gk_t
    grad_kv_ref[WIDTH:] = gv_t
    core = core_ref[0]
    ext_t = ext.astype(F32).T
    wt_ref[:WIDTH] = flip(wq_ref[...])
    wt_ref[WIDTH : 2 * WIDTH] = flip(wk)
    wt_ref[2 * WIDTH :] = flip(wv)
    x_mine, x_other = split_rows(ext_t[:, HALO : HALO + NODES], core)
    xt_ref[...] = x_mine.astype(BF)
    near_mine, near_other = split_rows(near_t[...], core)
    out_t_ref[...] = near_mine
    ext_t = ext_t.astype(BF)
    key_mine, key_other = split_rows(mm_nt(ext_t, gk_t), core)
    val_mine, val_other = split_rows(mm_nt(ext_t, gv_t), core)
    wkv_ref[0] = key_mine
    wkv_ref[1] = val_mine
    chip = [
        q_t, a_t, x_other, near_other, gq_t_ref[...], grad_ref[:, :NODES], grad_ref[:, NODES:],
        key_other[:, :NODES], key_other[:, NODES:], val_other[:, :NODES], val_other[:, NODES:],
    ]
    at = 0
    for part in chip:
        chip_ref[at : at + part.shape[0]] = part.astype(BF)
        at += part.shape[0]


def far_body(
    parts_ref, allowed_ref, both_ref, grad_ref, wq_ref, wk_ref, wv_ref, wt_ref,
    qt_ref, at_ref, xt_ref, near_t_ref, near_gq_ref, wkv_ref, core_ref,
    message_ref, gq_t_ref,
):
    core = core_ref[0]
    sibling = both_ref.at[1 - core]

    def section(i):
        return sibling[CHIP_AT[i] : CHIP_AT[i + 1]]

    def folded(i):
        rows = section(i)
        half = rows.shape[0] // 2
        return jnp.concatenate([rows[:half], rows[half:]], 1)

    heads = [rows_of(h) for h in range(HEADS)]
    wq = wq_ref[...]
    wk = wk_ref[...]
    wv = wv_ref[...]
    wt = wt_ref[...]
    totals = jnp.sum(parts_ref[...].astype(F32), 0)
    diagonal = iota((SUP, WIDTH), 0) == iota((SUP, WIDTH), 1)
    counts = jnp.sum(jnp.where(diagonal, totals[SUP : SUP + 1], 0.0), 1, keepdims=True)
    inverse = 1.0 / jnp.maximum(counts, 1.0)
    pooled = (totals[:SUP] * inverse).astype(BF)
    pooled_t = flip(pooled)

    s_proj_t = mm(wt, pooled_t).astype(BF)
    s_qt, s_kt, s_vt = (s_proj_t[i * WIDTH : (i + 1) * WIDTH] for i in range(3))
    s_k = mm(pooled, wk).astype(BF)
    s_v = mm(pooled, wv).astype(BF)
    allowed = allowed_ref[...]
    s_prob = [softmax_rows(mm(s_k[:, h], s_qt[h]) * SCORE_SCALE + allowed) for h in heads]
    s_weight = [p.astype(BF) for p in s_prob]
    moved_t = jnp.concatenate([mm(s_vt[h], w) for h, w in zip(heads, s_weight)], 0)
    state_t = pooled_t.astype(F32) + moved_t
    low_rank = jnp.concatenate(
        [split_rows(pooled_t.astype(F32), core)[0], split_rows(state_t, core)[0]], 1
    ).astype(BF)
    state_t = state_t.astype(BF)
    state = flip(state_t)

    c_proj_t = mm(wt[WIDTH:], state_t)
    c_kt = c_proj_t[:WIDTH].astype(BF)
    c_vt = split_rows(c_proj_t[WIDTH:], core)[0].astype(BF)
    c_k = mm(state, wk).astype(BF)
    c_v = mm(state, wv).astype(BF)
    q_t = jnp.concatenate([qt_ref[...], section(0)], 1)
    a_t = jnp.concatenate([at_ref[...], section(1)], 1)
    out_t = []
    gq_t = []
    gck_t = []
    gcv_t = []
    for i, h in enumerate(heads):
        prob = softmax_rows(mm(c_k[:, h], q_t[h]) * SCORE_SCALE)
        weight = prob.astype(BF)
        d_score = score_grad(prob, mm(c_v[:, h], a_t[h]))
        out_t.append(mm(c_vt[i * 16 : (i + 1) * 16], weight))
        gq_t.append(mm(c_kt[h], d_score))
        gck_t.append(mm_nt(q_t[h], d_score))
        gcv_t.append(mm_nt(a_t[h], weight))
    gck_t = jnp.concatenate(gck_t, 0).astype(BF)
    gcv_t = jnp.concatenate(gcv_t, 0).astype(BF)

    grad_state_t = mm(jnp.concatenate([wk, wv], 1), jnp.concatenate([gck_t, gcv_t], 0))
    gs_t = grad_state_t.astype(BF)
    gsq_t = []
    gsk_t = []
    gsv_t = []
    for h, prob, weight in zip(heads, s_prob, s_weight):
        d_score = score_grad(prob, mm(s_v[:, h], gs_t[h]))
        gsq_t.append(mm(s_kt[h], d_score))
        gsk_t.append(mm_nt(s_qt[h], d_score))
        gsv_t.append(mm_nt(gs_t[h], weight))
    gsq_t = jnp.concatenate(gsq_t, 0).astype(BF)
    gsk_t = jnp.concatenate(gsk_t, 0).astype(BF)
    gsv_t = jnp.concatenate(gsv_t, 0).astype(BF)
    grad_pooled_t = grad_state_t + mm(
        jnp.concatenate([wq, wk, wv], 1), jnp.concatenate([gsq_t, gsk_t, gsv_t], 0)
    )
    share = grad_pooled_t.T * inverse

    near_gq = jnp.concatenate([near_gq_ref[...], section(4).astype(F32)], 1)
    gq_t = (near_gq + jnp.concatenate(gq_t, 0)).astype(BF)
    gq_t_ref[...] = gq_t[:, :NODES]
    near_t = jnp.concatenate([near_t_ref[...], section(3).astype(F32)], 1)
    attended_t = (near_t + jnp.concatenate(out_t, 0)).astype(BF)
    x_t = jnp.concatenate([xt_ref[...], section(2)], 1)
    grad_out = jnp.concatenate([grad_ref[...], folded(5)], 0)
    near_kv = section(6).astype(F32)
    rows = near_kv.shape[0] // 4
    near_k = wkv_ref[0] + jnp.concatenate([near_kv[:rows], near_kv[rows : 2 * rows]], 1)
    near_v = wkv_ref[1] + jnp.concatenate([near_kv[2 * rows : 3 * rows], near_kv[3 * rows :]], 1)
    grads = [
        mm_nt(jnp.concatenate([x_t, low_rank[:, :SUP]], 1), jnp.concatenate([gq_t, gsq_t], 1)),
        near_k + mm_nt(low_rank, jnp.concatenate([gsk_t, gck_t], 1)),
        near_v + mm_nt(low_rank, jnp.concatenate([gsv_t, gcv_t], 1)),
        mm(attended_t, grad_out),
    ]
    half = SUP // 2
    first = jnp.broadcast_to(core, (half, WIDTH)) == 0
    pooled_half = jnp.where(first, share[:half], share[half:])
    quarter = half // len(grads)
    message_rows = message_ref.shape[1]
    n_z = message_ref.shape[0] // len(grads)
    own_rows = message_rows - quarter
    for w, grad in enumerate(grads):
        piece = pooled_half[w * quarter : (w + 1) * quarter]
        for z in range(n_z):
            rows = grad[z * own_rows : (z + 1) * own_rows]
            message_ref[w * n_z + z] = jnp.concatenate([rows, piece], 0).astype(BF)


def back_body(grad_kv_ref, grad_ref, wk_ref, wv_ref, base_ref, below_ref, above_ref):
    grad_kv = flip(grad_kv_ref[...])
    back = mm_nt(grad_kv[:, :WIDTH], wk_ref[...]) + mm_nt(grad_kv[:, WIDTH:], wv_ref[...])
    base_ref[...] = grad_ref[...].astype(F32) + back[HALO : HALO + NODES]
    below_ref[...] = back[:HALO].astype(BF)
    above_ref[...] = back[HALO + NODES :].astype(BF)


def own_body(base_ref, gq_t_ref, wq_ref, below_ref, above_ref, out_ref):
    own = base_ref[...] + mm_nt(flip(gq_t_ref[...]), wq_ref[...])
    out_ref[:HALO] = own[:HALO] + below_ref[...].astype(F32)
    out_ref[HALO : NODES - HALO] = own[HALO : NODES - HALO]
    out_ref[NODES - HALO :] = own[NODES - HALO :] + above_ref[...].astype(F32)


def shares_body(n_w, pieces_ref, own_ref, out_ref, pooled_ref):
    n_z = pieces_ref.shape[0] // n_w
    sums = [jnp.sum(pieces_ref[w * n_z : (w + 1) * n_z].astype(F32), 0) for w in range(n_w)]
    rows = out_ref.shape[1]
    share = sum(part[:rows] for part in sums).astype(BF)
    for y in range(out_ref.shape[0]):
        out_ref[y] = share
    pooled_ref[...] = jnp.concatenate([part[rows:] for part in sums], 0).astype(BF)


def columns_body(parts_ref, pooled_ref, out_ref):
    share = jnp.sum(parts_ref[...].astype(F32), 0)
    pooled = pooled_ref[...].astype(F32)
    n_w = out_ref.shape[0]
    quarter = pooled.shape[1] // n_w
    for w in range(n_w):
        rows = slice(w * quarter, (w + 1) * quarter)
        out_ref[w] = jnp.concatenate([share, pooled[0, rows], pooled[1, rows]], 0).astype(BF)


def final_body(scale, parts_ref, own_ref, cluster_ref, weights_ref, nodes_ref):
    n_w, rows, _ = weights_ref.shape
    quarter = (parts_ref.shape[1] - rows) // 2
    parts = parts_ref[...].astype(F32)
    weights_ref[...] = parts[:, :rows] * scale
    halves = [parts[w, rows + c * quarter : rows + (c + 1) * quarter] for c in range(2) for w in range(n_w)]
    pooled = jnp.concatenate(halves, 0).astype(BF)
    member = (cluster_ref[...] == iota((SUP, NODES), 0)).astype(F32).T.astype(BF)
    nodes_ref[...] = (own_ref[...] + mm(member, pooled)).astype(BF)


def swap(parts, axes):
    return lax.all_to_all(parts, axes, 0, 0, tiled=True)


def swap_back(parts, axes, count):
    order = [list(range(count))[::-1]]
    return lax.all_to_all(parts, axes, 0, 0, axis_index_groups=order, tiled=True)


def local(sizes, node_feats, grad_out, neighbours, cluster, super_links, w_query, w_key, w_value, w_out):
    n_x, n_y, n_z, n_c = sizes
    n_super = n_z * n_c
    n_dom = n_x * n_y
    supers = ("z", "c")
    up = [(i, (i + 1) % n_super) for i in range(n_super)]
    down = [(i, (i + n_super - 1) % n_super) for i in range(n_super)]
    cluster_row = cluster.reshape(1, NODES)
    sums, first_rows, last_rows, allowed = call(
        sums_body,
        "cluster_sums",
        [((n_z, SUM_ROWS, WIDTH), BF), ((HALO, WIDTH), BF), ((HALO, WIDTH), BF), ((SUP, SUP), F32)],
        [
            ((NODES, WIDTH), BF), ((1, NODES), jnp.int32), ((K_TOP, SUP), jnp.int32),
            pltpu.SemaphoreType.DMA((3,)),
        ],
        1 << 22,
        node_feats, cluster_row, super_links.T,
        outside=(0, 1, 2),
        vmem=60,
    )
    core = lax.axis_index("c").reshape(1)
    low = lax.ppermute(last_rows, supers, up)
    high = lax.ppermute(first_rows, supers, down)
    order = [[z // 2 if z % 2 == 0 else n_z - 1 - z // 2 for z in range(n_z)]]
    parts = lax.all_to_all(sums, "z", 0, 0, axis_index_groups=order, tiled=True)
    parts = lax.all_gather(parts, "c", tiled=True)
    q_t, a_t, x_t, w_t, near_t, near_gq, wkv, grad_kv, chip = call(
        near_body,
        "near_attention",
        [
            ((WIDTH, NODES), BF), ((WIDTH, NODES), BF), ((WIDTH // 2, NODES), BF), ((3 * WIDTH, WIDTH), BF),
            ((WIDTH // 2, NODES), F32), ((WIDTH, NODES), F32), ((2, WIDTH // 2, WIDTH), F32), ((2 * WIDTH, EXT), BF),
            ((CHIP_AT[-1], NODES), BF),
        ],
        [
            ((WIDTH, NODES), F32),
        ],
        10 << 30,
        low, node_feats, high, grad_out, neighbours.T, core, w_query, w_key, w_value, w_out,
    )
    base, below, above = call(
        back_body,
        "halo_returns",
        [((NODES, WIDTH), F32), ((HALO, WIDTH), BF), ((HALO, WIDTH), BF)],
        [],
        1 << 28,
        grad_kv, grad_out, w_key, w_value,
    )
    from_above = lax.ppermute(below, supers, down)
    from_below = lax.ppermute(above, supers, up)
    share_rows = WIDTH // n_super
    half = (SUP // 2, WIDTH)
    message_rows = share_rows + SUP // 2 // n_x
    pieces, gq_t = call(
        far_body,
        "far_attention",
        [((n_x * n_z, message_rows, WIDTH), BF), ((WIDTH, NODES), BF)],
        [],
        10 << 30,
        parts, allowed, lax.all_gather(chip, "c"), grad_out, w_query, w_key, w_value, w_t,
        q_t, a_t, x_t, near_t, near_gq, wkv, core,
    )
    pieces = swap(pieces, ("x", "z"))
    (own,) = call(
        own_body, "own_nodes", [((NODES, WIDTH), F32)], [], 1 << 28, base, gq_t, w_query, from_below, from_above
    )
    shares, pooled = call(
        functools.partial(shares_body, n_x),
        "weight_shares",
        [((n_y, share_rows, WIDTH), BF), (half, BF)],
        [],
        1 << 20,
        pieces, own,
        outside=(1,),
    )
    shares = swap_back(shares, "y", n_y)
    (columns,) = call(
        columns_body,
        "weight_columns",
        [((n_x, message_rows + SUP // 2 // n_x, WIDTH), BF)],
        [],
        1 << 20,
        shares, lax.all_gather(pooled, "c"),
    )
    columns = swap(columns, "x")
    scale = 1.0 / math.sqrt(NODES * n_super * n_dom)
    grad_weights, grad_nodes = call(
        functools.partial(final_body, scale),
        "gradients",
        [((4, share_rows, WIDTH), F32), ((NODES, WIDTH), BF)],
        [],
        1 << 20,
        columns, own, cluster_row,
    )
    return grad_nodes, grad_weights


def solution(mesh):
    n_dom = mesh.shape["dom"]
    n_super = mesh.shape["super"]
    sizes = (4, n_dom // 4, n_super // 2, 2)
    fine = Mesh(mesh.devices.reshape(sizes), ("x", "y", "z", "c"))
    everyone = ("x", "y", "z", "c")
    return jax.shard_map(
        functools.partial(local, sizes),
        mesh=fine,
        in_specs=(
            P(everyone, None),
            P(everyone, None),
            P(everyone, None),
            P(everyone),
            P(("x", "y"), None),
            P(),
            P(),
            P(),
            P(),
        ),
        out_specs=(P(everyone, None), P(None, ("z", "c"), None)),
        check_vma=False,
    )
```

```python
import functools
import math

import jax
import jax.numpy as jnp
from jax import lax
from jax.experimental import pallas as pl
from jax.experimental.pallas import tpu as pltpu
from jax.sharding import Mesh, PartitionSpec as P

WIDTH = 256
HEADS = 8
HEAD_DIM = 32
NODES = 128
HALO = 32
EXT = NODES + 2 * HALO
SUP = 64
K_TOP = 8
SUM_ROWS = SUP + 8
CHIP_ROWS = (256, 256, 128, 128, 256, 256, 512)
CHIP_AT = tuple(sum(CHIP_ROWS[:i]) for i in range(len(CHIP_ROWS) + 1))
SCORE_SCALE = 1.0 / math.sqrt(HEAD_DIM)
NEVER = -1e30
BF = jnp.bfloat16
F32 = jnp.float32


def mm(a, b):
    return jnp.dot(a, b, preferred_element_type=F32)


def mm_nt(a, b):
    return lax.dot_general(a, b, (((1,), (1,)), ((), ())), preferred_element_type=F32)


def iota(shape, dim):
    return lax.broadcasted_iota(jnp.int32, shape, dim)


def flip(a):
    return a.astype(F32).T.astype(a.dtype)


def rows_of(h):
    return slice(h * HEAD_DIM, (h + 1) * HEAD_DIM)


def split_rows(m, core):
    pairs = m.reshape(m.shape[0] // 32, 2, 16, m.shape[1])
    low, high = pairs[:, 0], pairs[:, 1]
    first = jnp.broadcast_to(core, low.shape) == 0
    shape = (m.shape[0] // 2, m.shape[1])
    return jnp.where(first, low, high).reshape(shape), jnp.where(first, high, low).reshape(shape)


def call(body, name, outs, scratch, flops, *args, outside=(), vmem=32):
    size = sum(a.size * a.dtype.itemsize for a in args)
    inside = pl.BlockSpec(memory_space=pltpu.VMEM)
    smem = pl.BlockSpec(memory_space=pltpu.SMEM)
    anywhere = pl.BlockSpec(memory_space=pltpu.HBM)
    return pl.pallas_call(
        body,
        in_specs=[anywhere if i in outside else smem if a.ndim == 1 else inside for i, a in enumerate(args)],
        name=name,
        out_shape=tuple(jax.ShapeDtypeStruct(s, d) for s, d in outs),
        scratch_shapes=[pltpu.VMEM(*s) if isinstance(s, tuple) else s for s in scratch],
        compiler_params=pltpu.CompilerParams(vmem_limit_bytes=vmem * 1024 * 1024),
        cost_estimate=pl.CostEstimate(flops=flops, bytes_accessed=size, transcendentals=0),
    )(*args)


def softmax_rows(scores):
    e = jnp.exp(scores)
    return e / jnp.sum(e, 0, keepdims=True)


def score_grad(prob, g):
    return (prob * (g - jnp.sum(prob * g, 0, keepdims=True)) * SCORE_SCALE).astype(BF)


def sums_body(
    x_any, cluster_any, links_any, out_ref, low_ref, high_ref, allowed_ref, x_ref, cluster_ref, links_ref, sems
):
    copies = [
        pltpu.make_async_copy(cluster_any, cluster_ref, sems.at[0]),
        pltpu.make_async_copy(x_any, x_ref, sems.at[1]),
        pltpu.make_async_copy(links_any, links_ref, sems.at[2]),
    ]
    for copy in copies:
        copy.start()
    for copy in copies:
        copy.wait()
    member = (cluster_ref[...] == iota((SUP, NODES), 0)).astype(F32)
    sums = mm(member.astype(BF), x_ref[...])
    counts = jnp.sum(member, 1, keepdims=True)
    diagonal = iota((SUP, WIDTH), 0) == iota((SUP, WIDTH), 1)
    count_row = jnp.sum(jnp.where(diagonal, counts, 0.0), 0, keepdims=True)
    count_rows = jnp.broadcast_to(count_row, (SUM_ROWS - SUP, WIDTH))
    message = jnp.concatenate([sums, count_rows], 0).astype(BF)
    for peer in range(out_ref.shape[0]):
        out_ref[peer] = message
    low_ref[...] = x_ref[:HALO]
    high_ref[...] = x_ref[NODES - HALO :]
    links = links_ref[...]
    target = iota((SUP, SUP), 0)
    linked = links[:1] == target
    for l in range(1, links.shape[0]):
        linked = jnp.logical_or(linked, links[l : l + 1] == target)
    allowed_ref[...] = jnp.where(linked, 0.0, NEVER)


def near_body(
    low_ref, x_ref, high_ref, grad_ref, slots_ref, core_ref, wq_ref, wk_ref, wv_ref, wo_ref,
    qt_ref, at_ref, xt_ref, wt_ref, out_t_ref, gq_t_ref, wkv_ref, grad_kv_ref, chip_ref,
    near_t,
):
    ext = jnp.concatenate([low_ref[...], x_ref[...], high_ref[...]], 0)
    wk = wk_ref[...]
    wv = wv_ref[...]
    queries = mm(x_ref[...], wq_ref[...]).astype(BF)
    keys = mm(ext, wk).astype(BF)
    vals = mm(ext, wv).astype(BF)
    grad_attn = mm_nt(grad_ref[...], wo_ref[...]).astype(BF)
    q_t = flip(queries)
    a_t = flip(grad_attn)
    keys_t = flip(keys)
    vals_t = flip(vals)
    qt_ref[...] = q_t
    at_ref[...] = a_t
    slots = slots_ref[...]
    row = iota((EXT, NODES), 0)
    count = jnp.zeros((EXT, NODES), F32)
    for j in range(slots.shape[0]):
        count = count + jnp.where(slots[j : j + 1] == row, 1.0, 0.0)
    log_count = jnp.where(count > 0.0, jnp.log(jnp.maximum(count, 1.0)), NEVER)
    gk_t = []
    gv_t = []
    for h in range(HEADS):
        rows = rows_of(h)
        prob = softmax_rows(mm(keys[:, rows], q_t[rows]) * SCORE_SCALE + log_count)
        weight = prob.astype(BF)
        d_score = score_grad(prob, mm(vals[:, rows], a_t[rows]))
        near_t[rows] = mm(vals_t[rows], weight)
        gq_t_ref[rows] = mm(keys_t[rows], d_score)
        gk_t.append(mm_nt(q_t[rows], d_score))
        gv_t.append(mm_nt(a_t[rows], weight))
    gk_t = jnp.concatenate(gk_t, 0).astype(BF)
    gv_t = jnp.concatenate(gv_t, 0).astype(BF)
    grad_kv_ref[:WIDTH] = gk_t
    grad_kv_ref[WIDTH:] = gv_t
    core = core_ref[0]
    ext_t = ext.astype(F32).T
    wt_ref[:WIDTH] = flip(wq_ref[...])
    wt_ref[WIDTH : 2 * WIDTH] = flip(wk)
    wt_ref[2 * WIDTH :] = flip(wv)
    x_mine, x_other = split_rows(ext_t[:, HALO : HALO + NODES], core)
    xt_ref[...] = x_mine.astype(BF)
    near_mine, near_other = split_rows(near_t[...], core)
    out_t_ref[...] = near_mine
    ext_t = ext_t.astype(BF)
    key_mine, key_other = split_rows(mm_nt(ext_t, gk_t), core)
    val_mine, val_other = split_rows(mm_nt(ext_t, gv_t), core)
    wkv_ref[0] = key_mine
    wkv_ref[1] = val_mine
    chip = [
        q_t, a_t, x_other, near_other, gq_t_ref[...], grad_ref[:, :NODES], grad_ref[:, NODES:],
        key_other[:, :NODES], key_other[:, NODES:], val_other[:, :NODES], val_other[:, NODES:],
    ]
    at = 0
    for part in chip:
        chip_ref[at : at + part.shape[0]] = part.astype(BF)
        at += part.shape[0]


def far_body(
    parts_ref, allowed_ref, both_ref, grad_ref, wq_ref, wk_ref, wv_ref, wt_ref,
    qt_ref, at_ref, xt_ref, near_t_ref, near_gq_ref, wkv_ref, core_ref,
    message_ref, gq_t_ref,
):
    core = core_ref[0]
    sibling = both_ref.at[1 - core]

    def section(i):
        return sibling[CHIP_AT[i] : CHIP_AT[i + 1]]

    def folded(i):
        rows = section(i)
        half = rows.shape[0] // 2
        return jnp.concatenate([rows[:half], rows[half:]], 1)

    heads = [rows_of(h) for h in range(HEADS)]
    wq = wq_ref[...]
    wk = wk_ref[...]
    wv = wv_ref[...]
    wt = wt_ref[...]
    totals = jnp.sum(parts_ref[...].astype(F32), 0)
    diagonal = iota((SUP, WIDTH), 0) == iota((SUP, WIDTH), 1)
    counts = jnp.sum(jnp.where(diagonal, totals[SUP : SUP + 1], 0.0), 1, keepdims=True)
    inverse = 1.0 / jnp.maximum(counts, 1.0)
    pooled = (totals[:SUP] * inverse).astype(BF)
    pooled_t = flip(pooled)

    s_proj_t = mm(wt, pooled_t).astype(BF)
    s_qt, s_kt, s_vt = (s_proj_t[i * WIDTH : (i + 1) * WIDTH] for i in range(3))
    s_k = mm(pooled, wk).astype(BF)
    s_v = mm(pooled, wv).astype(BF)
    allowed = allowed_ref[...]
    s_prob = [softmax_rows(mm(s_k[:, h], s_qt[h]) * SCORE_SCALE + allowed) for h in heads]
    s_weight = [p.astype(BF) for p in s_prob]
    moved_t = jnp.concatenate([mm(s_vt[h], w) for h, w in zip(heads, s_weight)], 0)
    state_t = pooled_t.astype(F32) + moved_t
    low_rank = jnp.concatenate(
        [split_rows(pooled_t.astype(F32), core)[0], split_rows(state_t, core)[0]], 1
    ).astype(BF)
    state_t = state_t.astype(BF)
    state = flip(state_t)

    c_proj_t = mm(wt[WIDTH:], state_t)
    c_kt = c_proj_t[:WIDTH].astype(BF)
    c_vt = split_rows(c_proj_t[WIDTH:], core)[0].astype(BF)
    c_k = mm(state, wk).astype(BF)
    c_v = mm(state, wv).astype(BF)
    q_t = jnp.concatenate([qt_ref[...], section(0)], 1)
    a_t = jnp.concatenate([at_ref[...], section(1)], 1)
    out_t = []
    gq_t = []
    gck_t = []
    gcv_t = []
    for i, h in enumerate(heads):
        prob = softmax_rows(mm(c_k[:, h], q_t[h]) * SCORE_SCALE)
        weight = prob.astype(BF)
        d_score = score_grad(prob, mm(c_v[:, h], a_t[h]))
        out_t.append(mm(c_vt[i * 16 : (i + 1) * 16], weight))
        gq_t.append(mm(c_kt[h], d_score))
        gck_t.append(mm_nt(q_t[h], d_score))
        gcv_t.append(mm_nt(a_t[h], weight))
    gck_t = jnp.concatenate(gck_t, 0).astype(BF)
    gcv_t = jnp.concatenate(gcv_t, 0).astype(BF)

    grad_state_t = mm(jnp.concatenate([wk, wv], 1), jnp.concatenate([gck_t, gcv_t], 0))
    gs_t = grad_state_t.astype(BF)
    gsq_t = []
    gsk_t = []
    gsv_t = []
    for h, prob, weight in zip(heads, s_prob, s_weight):
        d_score = score_grad(prob, mm(s_v[:, h], gs_t[h]))
        gsq_t.append(mm(s_kt[h], d_score))
        gsk_t.append(mm_nt(s_qt[h], d_score))
        gsv_t.append(mm_nt(gs_t[h], weight))
    gsq_t = jnp.concatenate(gsq_t, 0).astype(BF)
    gsk_t = jnp.concatenate(gsk_t, 0).astype(BF)
    gsv_t = jnp.concatenate(gsv_t, 0).astype(BF)
    grad_pooled_t = grad_state_t + mm(
        jnp.concatenate([wq, wk, wv], 1), jnp.concatenate([gsq_t, gsk_t, gsv_t], 0)
    )
    share = grad_pooled_t.T * inverse

    near_gq = jnp.concatenate([near_gq_ref[...], section(4).astype(F32)], 1)
    gq_t = (near_gq + jnp.concatenate(gq_t, 0)).astype(BF)
    gq_t_ref[...] = gq_t[:, :NODES]
    near_t = jnp.concatenate([near_t_ref[...], section(3).astype(F32)], 1)
    attended_t = (near_t + jnp.concatenate(out_t, 0)).astype(BF)
    x_t = jnp.concatenate([xt_ref[...], section(2)], 1)
    grad_out = jnp.concatenate([grad_ref[...], folded(5)], 0)
    near_kv = section(6).astype(F32)
    rows = near_kv.shape[0] // 4
    near_k = wkv_ref[0] + jnp.concatenate([near_kv[:rows], near_kv[rows : 2 * rows]], 1)
    near_v = wkv_ref[1] + jnp.concatenate([near_kv[2 * rows : 3 * rows], near_kv[3 * rows :]], 1)
    grads = [
        mm_nt(jnp.concatenate([x_t, low_rank[:, :SUP]], 1), jnp.concatenate([gq_t, gsq_t], 1)),
        near_k + mm_nt(low_rank, jnp.concatenate([gsk_t, gck_t], 1)),
        near_v + mm_nt(low_rank, jnp.concatenate([gsv_t, gcv_t], 1)),
        mm(attended_t, grad_out),
    ]
    half = SUP // 2
    first = jnp.broadcast_to(core, (half, WIDTH)) == 0
    pooled_half = jnp.where(first, share[:half], share[half:])
    quarter = half // len(grads)
    message_rows = message_ref.shape[1]
    n_z = message_ref.shape[0] // len(grads)
    own_rows = message_rows - quarter
    for w, grad in enumerate(grads):
        piece = pooled_half[w * quarter : (w + 1) * quarter]
        for z in range(n_z):
            rows = grad[z * own_rows : (z + 1) * own_rows]
            message_ref[w * n_z + z] = jnp.concatenate([rows, piece], 0).astype(BF)


def back_body(grad_kv_ref, grad_ref, wk_ref, wv_ref, base_ref, below_ref, above_ref):
    grad_kv = flip(grad_kv_ref[...])
    back = mm_nt(grad_kv[:, :WIDTH], wk_ref[...]) + mm_nt(grad_kv[:, WIDTH:], wv_ref[...])
    base_ref[...] = grad_ref[...].astype(F32) + back[HALO : HALO + NODES]
    below_ref[...] = back[:HALO].astype(BF)
    above_ref[...] = back[HALO + NODES :].astype(BF)


def own_body(base_ref, gq_t_ref, wq_ref, below_ref, above_ref, out_ref):
    own = base_ref[...] + mm_nt(flip(gq_t_ref[...]), wq_ref[...])
    out_ref[:HALO] = own[:HALO] + below_ref[...].astype(F32)
    out_ref[HALO : NODES - HALO] = own[HALO : NODES - HALO]
    out_ref[NODES - HALO :] = own[NODES - HALO :] + above_ref[...].astype(F32)


def shares_body(n_w, pieces_ref, own_ref, out_ref, pooled_ref):
    n_z = pieces_ref.shape[0] // n_w
    sums = [jnp.sum(pieces_ref[w * n_z : (w + 1) * n_z].astype(F32), 0) for w in range(n_w)]
    rows = out_ref.shape[1]
    share = sum(part[:rows] for part in sums).astype(BF)
    for y in range(out_ref.shape[0]):
        out_ref[y] = share
    pooled_ref[...] = jnp.concatenate([part[rows:] for part in sums], 0).astype(BF)


def columns_body(parts_ref, pooled_ref, out_ref):
    share = jnp.sum(parts_ref[...].astype(F32), 0)
    pooled = pooled_ref[...].astype(F32)
    n_w = out_ref.shape[0]
    quarter = pooled.shape[1] // n_w
    for w in range(n_w):
        rows = slice(w * quarter, (w + 1) * quarter)
        out_ref[w] = jnp.concatenate([share, pooled[0, rows], pooled[1, rows]], 0).astype(BF)


def final_body(scale, parts_ref, own_ref, cluster_ref, weights_ref, nodes_ref):
    n_w, rows, _ = weights_ref.shape
    quarter = (parts_ref.shape[1] - rows) // 2
    parts = parts_ref[...].astype(F32)
    weights_ref[...] = parts[:, :rows] * scale
    halves = [parts[w, rows + c * quarter : rows + (c + 1) * quarter] for c in range(2) for w in range(n_w)]
    pooled = jnp.concatenate(halves, 0).astype(BF)
    member = (cluster_ref[...] == iota((SUP, NODES), 0)).astype(F32).T.astype(BF)
    nodes_ref[...] = (own_ref[...] + mm(member, pooled)).astype(BF)


def swap(parts, axes):
    return lax.all_to_all(parts, axes, 0, 0, tiled=True)


def swap_back(parts, axes, count):
    order = [list(range(count // 2, count)) + list(range(count // 2))[::-1]]
    return lax.all_to_all(parts, axes, 0, 0, axis_index_groups=order, tiled=True)


def local(sizes, node_feats, grad_out, neighbours, cluster, super_links, w_query, w_key, w_value, w_out):
    n_x, n_y, n_z, n_c = sizes
    n_super = n_z * n_c
    n_dom = n_x * n_y
    supers = ("z", "c")
    up = [(i, (i + 1) % n_super) for i in range(n_super)]
    down = [(i, (i + n_super - 1) % n_super) for i in range(n_super)]
    cluster_row = cluster.reshape(1, NODES)
    sums, first_rows, last_rows, allowed = call(
        sums_body,
        "cluster_sums",
        [((n_z, SUM_ROWS, WIDTH), BF), ((HALO, WIDTH), BF), ((HALO, WIDTH), BF), ((SUP, SUP), F32)],
        [
            ((NODES, WIDTH), BF), ((1, NODES), jnp.int32), ((K_TOP, SUP), jnp.int32),
            pltpu.SemaphoreType.DMA((3,)),
        ],
        1 << 22,
        node_feats, cluster_row, super_links.T,
        outside=(0, 1, 2),
        vmem=60,
    )
    core = lax.axis_index("c").reshape(1)
    low = lax.ppermute(last_rows, supers, up)
    high = lax.ppermute(first_rows, supers, down)
    order = [[z // 2 if z % 2 == 0 else n_z - 1 - z // 2 for z in range(n_z)]]
    parts = lax.all_to_all(sums, "z", 0, 0, axis_index_groups=order, tiled=True)
    parts = lax.all_gather(parts, "c", tiled=True)
    q_t, a_t, x_t, w_t, near_t, near_gq, wkv, grad_kv, chip = call(
        near_body,
        "near_attention",
        [
            ((WIDTH, NODES), BF), ((WIDTH, NODES), BF), ((WIDTH // 2, NODES), BF), ((3 * WIDTH, WIDTH), BF),
            ((WIDTH // 2, NODES), F32), ((WIDTH, NODES), F32), ((2, WIDTH // 2, WIDTH), F32), ((2 * WIDTH, EXT), BF),
            ((CHIP_AT[-1], NODES), BF),
        ],
        [
            ((WIDTH, NODES), F32),
        ],
        10 << 30,
        low, node_feats, high, grad_out, neighbours.T, core, w_query, w_key, w_value, w_out,
    )
    base, below, above = call(
        back_body,
        "halo_returns",
        [((NODES, WIDTH), F32), ((HALO, WIDTH), BF), ((HALO, WIDTH), BF)],
        [],
        1 << 28,
        grad_kv, grad_out, w_key, w_value,
    )
    from_above = lax.ppermute(below, supers, down)
    from_below = lax.ppermute(above, supers, up)
    share_rows = WIDTH // n_super
    half = (SUP // 2, WIDTH)
    message_rows = share_rows + SUP // 2 // n_x
    pieces, gq_t = call(
        far_body,
        "far_attention",
        [((n_x * n_z, message_rows, WIDTH), BF), ((WIDTH, NODES), BF)],
        [],
        10 << 30,
        parts, allowed, lax.all_gather(chip, "c"), grad_out, w_query, w_key, w_value, w_t,
        q_t, a_t, x_t, near_t, near_gq, wkv, core,
    )
    pieces = swap(pieces, ("x", "z"))
    (own,) = call(
        own_body, "own_nodes", [((NODES, WIDTH), F32)], [], 1 << 28, base, gq_t, w_query, from_below, from_above
    )
    shares, pooled = call(
        functools.partial(shares_body, n_x),
        "weight_shares",
        [((n_y, share_rows, WIDTH), BF), (half, BF)],
        [],
        1 << 20,
        pieces, own,
        outside=(1,),
    )
    shares = swap_back(shares, "y", n_y)
    (columns,) = call(
        columns_body,
        "weight_columns",
        [((n_x, message_rows + SUP // 2 // n_x, WIDTH), BF)],
        [],
        1 << 20,
        shares, lax.all_gather(pooled, "c"),
    )
    columns = swap(columns, "x")
    scale = 1.0 / math.sqrt(NODES * n_super * n_dom)
    grad_weights, grad_nodes = call(
        functools.partial(final_body, scale),
        "gradients",
        [((4, share_rows, WIDTH), F32), ((NODES, WIDTH), BF)],
        [],
        1 << 20,
        columns, own, cluster_row,
    )
    return grad_nodes, grad_weights


def solution(mesh):
    n_dom = mesh.shape["dom"]
    n_super = mesh.shape["super"]
    sizes = (4, n_dom // 4, n_super // 2, 2)
    fine = Mesh(mesh.devices.reshape(sizes), ("x", "y", "z", "c"))
    everyone = ("x", "y", "z", "c")
    return jax.shard_map(
        functools.partial(local, sizes),
        mesh=fine,
        in_specs=(
            P(everyone, None),
            P(everyone, None),
            P(everyone, None),
            P(everyone),
            P(("x", "y"), None),
            P(),
            P(),
            P(),
            P(),
        ),
        out_specs=(P(everyone, None), P(None, ("z", "c"), None)),
        check_vma=False,
    )
```
